32 devices in a mesh: ctx: 8 (over z, core), head: 4 (over y, x).
Axes of the slice: x: 2, y: 2, z: 4, core: 2. Of those that a mesh axis runs over, the one named last changes fastest.
Arguments:
- attn_q: bfloat16 [1024, 4096], P('ctx', 'head'), may hold values from -6 to 6
- attn_k: bfloat16 [1024, 512], P('ctx'), may hold values from -6 to 6
- attn_v: bfloat16 [1024, 512], P('ctx'), may hold values from -0.375 to 0.375
- attn_cot: bfloat16 [1024, 4096], P('ctx', 'head'), may hold values from -6 to 6
- attn_lse: float32 [16, 1024], P('head'), may hold values from 3 to 6
- attn_delta: float32 [16, 1024], P('head'), may hold values from -6 to 6
- block_lists: int32 [16, 16, 4], P('head'), may hold values from 0 to 15, as said below
- gdn_q: bfloat16 [1024, 2048], P('ctx', 'head'), may hold values from -6 to 6
- gdn_k: bfloat16 [1024, 2048], P('ctx', 'head'), may hold values from -6 to 6
- gdn_v: bfloat16 [1024, 4096], P('ctx', 'head'), may hold values from -6 to 6
- decay_logit: float32 [32, 1024], P('head', 'ctx'), may hold values from -8 to 8
- write_logit: float32 [32, 1024], P('head', 'ctx'), may hold values from -6 to 6
- decay_rate: float32 [32], P('head'), may hold values from 0.0009765625 to 0.1
- write_scale: float32 [32], P('head'), may hold values from 0.05 to 1
- gdn_cot: bfloat16 [1024, 4096], P('ctx', 'head'), may hold values from -6 to 6
Outputs:
- attn_dq: float32 [1024, 4096], P('ctx', 'head')
- attn_dk: float32 [1024, 512], P('ctx')
- attn_dv: float32 [1024, 512], P('ctx')
- gdn_dq: float32 [1024, 2048], P('ctx', 'head')
- gdn_dk: float32 [1024, 2048], P('ctx', 'head')
- gdn_dv: float32 [1024, 4096], P('ctx', 'head')
- gdn_ddecay: float32 [32, 1024], P('head', 'ctx')
- gdn_dwrite: float32 [32, 1024], P('head', 'ctx')
The draws below stay inside these ranges and needn't reach their ends.
Inputs may be any that keep to these rules, and one draw needn't show every extreme that they name: `block_lists`: entries for query block b lie in 0 to b and may repeat.
All inputs are finite; a program needn't handle non-finite values.
Results may differ from the reference program's by a relative error of at most 0.00035.
Values may be sent and summed in bfloat16 or wider, within the bound.
A program may use at most 128 MiB of HBM per device.

```python
import math
import jax
import jax.numpy as jnp
from jax import lax

Q_HEADS = 16
KV_HEADS = 2
HD = 256
GK_HEADS = 16
GV_HEADS = 32
GDIM = 128
BLK = 64
TOPK = 4
SPAN = 64
TOKENS = 1024


def draw_block_lists(key, part):
    n_blocks = TOKENS // BLK
    upper_bound = jnp.arange(1, n_blocks + 1, dtype=jnp.int32)[None, :, None]
    return jax.random.randint(key, (Q_HEADS, n_blocks, TOPK), 0, upper_bound, dtype=jnp.int32)


def block_levels(rng, dims, pieces, low, top_value):
    loudness = 1.0
    for dim, shards_of in pieces:
        draws = jax.random.uniform(jax.random.fold_in(jax.random.fold_in(rng, 6), dim), (shards_of,), jnp.float32, low / len(pieces), top_value / len(pieces))
        loudness = loudness * jnp.repeat(jnp.exp(draws), dims[dim] // shards_of).reshape((-1,) + (1,) * (len(dims) - 1 - dim))
    return loudness


def gaussian(key, dims, width, reach, pieces=(), kind=jnp.bfloat16):
    result = width * jax.random.normal(key, dims, jnp.float32)
    if pieces:
        result = result * block_levels(key, dims, pieces, -0.22, 0.18)
    return jnp.clip(result, -reach, reach).astype(kind)


def setup_inputs(seed: int = 0) -> dict:
    seeds = jax.random.split(jax.random.key(seed), 16)
    attn_q = gaussian(seeds[0], (TOKENS, Q_HEADS * HD), 1.0, 6.0, ((0, 8), (1, 4)))
    attn_k = gaussian(seeds[1], (TOKENS, KV_HEADS * HD), 1.0, 6.0, ((0, 8),))
    attn_v = gaussian(seeds[2], (TOKENS, KV_HEADS * HD), 0.0625, 0.375, ((0, 8),))
    attn_cot = gaussian(seeds[3], (TOKENS, Q_HEADS * HD), 1.0, 6.0, ((0, 8), (1, 4)))
    attn_lse = jnp.clip(3.0 + 3.0 * jax.random.uniform(seeds[4], (Q_HEADS, TOKENS), jnp.float32) ** block_levels(seeds[4], (Q_HEADS, TOKENS), ((0, 4),), -0.2, 0.2), 3.0, 6.0)
    attn_delta = gaussian(seeds[5], (Q_HEADS, TOKENS), 1.0, 6.0, ((0, 4),), jnp.float32)
    block_lists = draw_block_lists(jax.random.fold_in(seeds[15], 71), 0)
    gdn_q = gaussian(seeds[7], (TOKENS, GK_HEADS * GDIM), 1.0, 6.0, ((0, 8), (1, 4)))
    gdn_k = gaussian(seeds[8], (TOKENS, GK_HEADS * GDIM), 1.0, 6.0, ((0, 8), (1, 4)))
    gdn_v = gaussian(seeds[9], (TOKENS, GV_HEADS * GDIM), 1.0, 6.0, ((0, 8), (1, 4)))
    decay_logit = gaussian(seeds[10], (GV_HEADS, TOKENS), 1.5, 8.0, ((0, 4), (1, 8)), jnp.float32)
    write_logit = gaussian(seeds[11], (GV_HEADS, TOKENS), 1.0, 6.0, ((0, 4), (1, 8)), jnp.float32)
    decay_rate = jnp.clip(jnp.exp(math.log(0.1) - 4.6288867 * jax.random.uniform(seeds[12], (GV_HEADS,), jnp.float32) ** block_levels(seeds[12], (GV_HEADS,), ((0, 4),), -0.2, 0.2)), 0.0009765625, 0.1)
    write_scale = jnp.clip(jnp.exp(math.log(1.0) - 2.9957323 * jax.random.uniform(seeds[13], (GV_HEADS,), jnp.float32) ** block_levels(seeds[13], (GV_HEADS,), ((0, 4),), -0.2, 0.2)), 0.05, 1.0)
    gdn_cot = gaussian(seeds[14], (TOKENS, GV_HEADS * GDIM), 1.0, 6.0, ((0, 8), (1, 4)))
    return {"attn_q": attn_q, "attn_k": attn_k, "attn_v": attn_v, "attn_cot": attn_cot, "attn_lse": attn_lse, "attn_delta": attn_delta, "block_lists": block_lists, "gdn_q": gdn_q, "gdn_k": gdn_k, "gdn_v": gdn_v, "decay_logit": decay_logit, "write_logit": write_logit, "decay_rate": decay_rate, "write_scale": write_scale, "gdn_cot": gdn_cot}


HIGHEST = lax.Precision.HIGHEST

def unit_rows(matrix):
    return matrix / jnp.sqrt(lax.optimization_barrier(jnp.sum(matrix * matrix, axis=-1, keepdims=True)) + 1e-06)

def span_update(memory, packed):
    queries, keys_in, values_in, log_decay, write_gain = packed
    length = log_decay.shape[-1]
    cum_log = jnp.cumsum(log_decay, axis=-1)
    log_gap = cum_log[:, :, None] - cum_log[:, None, :]
    order_ids = jnp.arange(length)
    strict_low = order_ids[:, None] > order_ids[None, :]
    with_diag = order_ids[:, None] >= order_ids[None, :]
    decay_strict = jnp.where(strict_low, jnp.exp(jnp.where(strict_low, log_gap, 0.0)), 0.0)
    decay_upto = jnp.where(with_diag, jnp.exp(jnp.where(with_diag, log_gap, 0.0)), 0.0)
    key_gram = jnp.einsum('htd,hsd->hts', keys_in, keys_in, precision=HIGHEST)
    system = write_gain[:, :, None] * decay_strict * key_gram + jnp.eye(length, dtype=jnp.float32)
    decay_now = jnp.exp(cum_log)
    recalled = jnp.einsum('hvd,htd->htv', memory, keys_in, precision=HIGHEST)
    target = write_gain[:, :, None] * (values_in - decay_now[:, :, None] * recalled)
    written = lax.linalg.triangular_solve(system, target, left_side=True, lower=True, unit_diagonal=True)
    read_old = jnp.einsum('hvd,htd->htv', memory, queries, precision=HIGHEST)
    query_key = jnp.einsum('htd,hsd->hts', queries, keys_in, precision=HIGHEST)
    outputs = decay_now[:, :, None] * read_old + jnp.einsum('hts,hsv->htv', decay_upto * query_key, written, precision=HIGHEST)
    tail_decay = jnp.exp(cum_log[:, -1:] - cum_log)
    memory_next = jnp.exp(cum_log[:, -1])[:, None, None] * memory + jnp.einsum('hsv,hsd->hvd', written * tail_decay[:, :, None], keys_in, precision=HIGHEST)
    return (memory_next, outputs)

def delta_forward(raw_inputs, memory, rate_heads, scale_heads):
    query_raw, key_raw, value_raw, decay_in, write_in = raw_inputs
    n_tokens = query_raw.shape[0]
    key_heads = query_raw.shape[1] // GDIM
    value_heads = value_raw.shape[1] // GDIM
    ratio_heads = value_heads // key_heads
    n_spans = n_tokens // SPAN
    queries = jnp.repeat(unit_rows(query_raw.reshape(n_tokens, key_heads, GDIM)), ratio_heads, axis=1)
    keys_norm = jnp.repeat(unit_rows(key_raw.reshape(n_tokens, key_heads, GDIM)), ratio_heads, axis=1)
    values_in = value_raw.reshape(n_tokens, value_heads, GDIM)
    log_decay = -rate_heads[:, None] * jax.nn.softplus(decay_in)
    write_gain = scale_heads[:, None] * jax.nn.sigmoid(write_in)

    def blocks_of(tensor):
        return tensor.reshape(n_spans, SPAN, value_heads, GDIM).transpose(0, 2, 1, 3)

    def gates_of(tensor):
        return tensor.reshape(value_heads, n_spans, SPAN).transpose(1, 0, 2)
    memory_end, outputs = lax.scan(span_update, memory, (blocks_of(queries), blocks_of(keys_norm), blocks_of(values_in), gates_of(log_decay), gates_of(write_gain)))
    return (outputs.transpose(0, 2, 1, 3).reshape(n_tokens, value_heads * GDIM), memory_end)

def sparse_terms(q_blocks, cot_blocks, own_keys, own_values, listed_keys, listed_values, lse_rows, delta_rows, head_lists, block_ids):
    score_scale = HD ** (-0.5)
    q_full = q_blocks.astype(jnp.float32)
    cot_full = cot_blocks.astype(jnp.float32)
    own_kf = own_keys.astype(jnp.float32)
    own_vf = own_values.astype(jnp.float32)
    list_kf = listed_keys.astype(jnp.float32)
    list_vf = listed_values.astype(jnp.float32)
    position = jnp.arange(BLK)
    causal = position[:, None] >= position[None, :]
    slot_ids = jnp.arange(TOPK)
    repeated = jnp.any((head_lists[:, :, None] == head_lists[:, None, :]) & (slot_ids[:, None] > slot_ids[None, :]), axis=2)
    usable = (head_lists < block_ids[:, None]) & jnp.logical_not(repeated)
    own_score = jnp.einsum('bid,bjd->bij', q_full, own_kf, precision=HIGHEST) * score_scale
    list_score = jnp.einsum('bid,btjd->bitj', q_full, list_kf, precision=HIGHEST) * score_scale
    own_prob = jnp.where(causal[None], jnp.exp(own_score - lse_rows[:, :, None]), 0.0)
    list_prob = jnp.where(usable[:, None, :, None], jnp.exp(list_score - lse_rows[:, :, None, None]), 0.0)
    own_dprob = jnp.einsum('bid,bjd->bij', cot_full, own_vf, precision=HIGHEST)
    list_dprob = jnp.einsum('bid,btjd->bitj', cot_full, list_vf, precision=HIGHEST)
    own_dscore = own_prob * (own_dprob - delta_rows[:, :, None])
    list_dscore = list_prob * (list_dprob - delta_rows[:, :, None, None])
    grad_query = (jnp.einsum('bij,bjd->bid', own_dscore, own_kf, precision=HIGHEST) + jnp.einsum('bitj,btjd->bid', list_dscore, list_kf, precision=HIGHEST)) * score_scale
    own_gk = jnp.einsum('bij,bid->bjd', own_dscore, q_full, precision=HIGHEST) * score_scale
    list_gk = jnp.einsum('bitj,bid->btjd', list_dscore, q_full, precision=HIGHEST) * score_scale
    own_gv = jnp.einsum('bij,bid->bjd', own_prob, cot_full, precision=HIGHEST)
    list_gv = jnp.einsum('bitj,bid->btjd', list_prob, cot_full, precision=HIGHEST)
    return (grad_query, own_gk, list_gk, own_gv, list_gv)

def attention_grads(attn_q, attn_k, attn_v, attn_cot, attn_lse, attn_delta, block_lists):
    n_blocks = TOKENS // BLK
    group_size = Q_HEADS // KV_HEADS
    block_ids = jnp.arange(n_blocks, dtype=jnp.int32)
    key_blocks = attn_k.reshape(n_blocks, BLK, KV_HEADS, HD).transpose(2, 0, 1, 3)
    value_blocks = attn_v.reshape(n_blocks, BLK, KV_HEADS, HD).transpose(2, 0, 1, 3)

    def per_head(packed):
        head_q, head_cot, head_lse, head_delta, head_lists, kv_index = packed
        head_keys = lax.dynamic_index_in_dim(key_blocks, kv_index, 0, keepdims=False)
        head_values = lax.dynamic_index_in_dim(value_blocks, kv_index, 0, keepdims=False)
        grad_query, own_gk, list_gk, own_gv, list_gv = sparse_terms(head_q, head_cot, head_keys, head_values, head_keys[head_lists], head_values[head_lists], head_lse, head_delta, head_lists, block_ids)
        grad_key = own_gk.at[head_lists].add(list_gk)
        grad_value = own_gv.at[head_lists].add(list_gv)
        return (grad_query.reshape(TOKENS, HD), grad_key.reshape(TOKENS, HD), grad_value.reshape(TOKENS, HD))
    q_heads = attn_q.reshape(n_blocks, BLK, Q_HEADS, HD).transpose(2, 0, 1, 3)
    cot_heads = attn_cot.reshape(n_blocks, BLK, Q_HEADS, HD).transpose(2, 0, 1, 3)
    kv_index = (jnp.arange(Q_HEADS) // group_size).astype(jnp.int32)
    grad_query, grad_key, grad_value = lax.map(per_head, (q_heads, cot_heads, attn_lse.reshape(Q_HEADS, n_blocks, BLK), attn_delta.reshape(Q_HEADS, n_blocks, BLK), block_lists, kv_index))
    attn_dq = grad_query.transpose(1, 0, 2).reshape(TOKENS, Q_HEADS * HD)
    attn_dk = grad_key.reshape(KV_HEADS, group_size, TOKENS, HD).sum(axis=1).transpose(1, 0, 2).reshape(TOKENS, KV_HEADS * HD)
    attn_dv = grad_value.reshape(KV_HEADS, group_size, TOKENS, HD).sum(axis=1).transpose(1, 0, 2).reshape(TOKENS, KV_HEADS * HD)
    return (attn_dq, attn_dk, attn_dv)

def reference(attn_q, attn_k, attn_v, attn_cot, attn_lse, attn_delta, block_lists, gdn_q, gdn_k, gdn_v, decay_logit, write_logit, decay_rate, write_scale, gdn_cot):
    attn_dq, attn_dk, attn_dv = attention_grads(attn_q, attn_k, attn_v, attn_cot, attn_lse, attn_delta, block_lists)
    raw_inputs = (gdn_q.astype(jnp.float32), gdn_k.astype(jnp.float32), gdn_v.astype(jnp.float32), decay_logit.astype(jnp.float32), write_logit.astype(jnp.float32))
    start_memory = jnp.zeros((GV_HEADS, GDIM, GDIM), jnp.float32)

    def run_layer(raw_values):
        return delta_forward(raw_values, start_memory, decay_rate, write_scale)[0]
    unused_out, pullback = jax.vjp(run_layer, raw_inputs)
    grads = pullback(gdn_cot.astype(jnp.float32))[0]
    return (attn_dq, attn_dk, attn_dv, grads[0], grads[1], grads[2], grads[3], grads[4])
```

```python
import jax
import jax.numpy as jnp
from jax import lax
from jax.experimental import pallas as pl
from jax.experimental.pallas import tpu as pltpu
from jax.sharding import PartitionSpec as P

Q_HEADS = 16
KV_HEADS = 2
HD = 256
GDIM = 128
BLK = 64
TOPK = 4
F32 = jnp.float32
BF16 = jnp.bfloat16
VMEM_BYTES = 48 * 1024 * 1024
MESH = pl.DeviceIdType.MESH


def split(x):
    if x.dtype == BF16:
        return (x, None)
    head = x.astype(BF16)
    return (head, (x - head.astype(F32)).astype(BF16))


def mm(a, b, ca=1, cb=0):
    dims = (((ca,), (cb,)), ((), ()))
    out = lax.dot_general(a[0], b[0], dims, preferred_element_type=F32)
    if b[1] is not None:
        out = out + lax.dot_general(a[0], b[1], dims, preferred_element_type=F32)
    if a[1] is not None:
        out = out + lax.dot_general(a[1], b[0], dims, preferred_element_type=F32)
    return out


def lane_cumsum(x, backward):
    width = x.shape[1]
    lanes = lax.broadcasted_iota(jnp.int32, x.shape, 1)
    step = 1
    while step < width:
        moved = pltpu.roll(x, width - step if backward else step, 1)
        keep = lanes < width - step if backward else lanes >= step
        x = x + jnp.where(keep, moved, 0.0)
        step *= 2
    return x


def softplus(x):
    return jnp.maximum(x, 0.0) + jnp.log(1.0 + jnp.exp(-jnp.abs(x)))


def sigmoid(x):
    return 1.0 / (1.0 + jnp.exp(-x))


def column_form(row, size):
    return jnp.broadcast_to(row, (size, size)).T


def unit_rows(raw):
    full = raw.astype(F32)
    scale = lax.rsqrt(jnp.sum(full * full, axis=-1, keepdims=True) + 1e-06)
    return full * scale, scale


def head_cols(ref, head):
    return ref[:, head * GDIM : (head + 1) * GDIM]


def triangles(size):
    rows = lax.broadcasted_iota(jnp.int32, (size, size), 0)
    cols = lax.broadcasted_iota(jnp.int32, (size, size), 1)
    return rows, cols


def gdn_local(
    q_ref, k_ref, v_ref, cot_ref, decay_ref, write_ref, rate_ref, scale_ref,
    inv_ref, wu_ref, map_ref, mapt_ref, add_ref, pull_ref, gam_ref, beta_ref,
):
    size = q_ref.shape[0]
    key_heads = q_ref.shape[1] // GDIM
    value_heads = v_ref.shape[1] // GDIM
    ratio = value_heads // key_heads
    gam = lane_cumsum(-rate_ref[...] * softplus(decay_ref[...]), False)
    beta = scale_ref[...] * sigmoid(write_ref[...])
    gam_ref[...] = gam
    beta_ref[...] = beta
    rows, cols = triangles(size)
    eye = jnp.where(rows == cols, 1.0, 0.0)
    group = min(4, value_heads)
    for first in range(0, value_heads, group):
        heads = list(range(first, first + group))
        keyed = {}
        for m in sorted({v // ratio for v in heads}):
            qn, kn = unit_rows(head_cols(q_ref, m))[0], unit_rows(head_cols(k_ref, m))[0]
            qs, ks = split(qn), split(kn)
            keyed[m] = (qn, kn, mm(ks, ks, 1, 1), mm(qs, ks, 1, 1), split(kn.T))
        gcol = [column_form(gam[v : v + 1, :], size) for v in heads]
        bcol = [column_form(beta[v : v + 1, :], size) for v in heads]
        upto = [
            jnp.where(rows >= cols, jnp.exp(jnp.minimum(c - gam[v : v + 1, :], 0.0)), 0.0)
            for c, v in zip(gcol, heads)
        ]
        system = [
            jnp.where(rows > cols, b * u * keyed[v // ratio][2], 0.0)
            for b, u, v in zip(bcol, upto, heads)
        ]
        inverse = [eye - jnp.where(rows // 2 == cols // 2, s, 0.0) for s in system]
        half = 2
        while half < size:
            low = (rows // half == cols // half + 1) & ((rows // half) % 2 == 1)
            parts = [split(t) for t in inverse]
            inner = [mm(split(jnp.where(low, s, 0.0)), t) for s, t in zip(system, parts)]
            outer = [mm(t, split(x)) for t, x in zip(parts, inner)]
            inverse = [t - x for t, x in zip(inverse, outer)]
            half *= 2
        for n, v in enumerate(heads):
            qn, kn, gram, cross, knt = keyed[v // ratio]
            now = jnp.exp(gcol[n])
            inv_ref[v] = inverse[n]
            targets = jnp.concatenate(
                [bcol[n] * now * kn, bcol[n] * head_cols(v_ref, v).astype(F32)], axis=1
            )
            wu = mm(split(inverse[n]), split(targets))
            wu_ref[v] = wu
            last = gam[v : v + 1, size - 1 : size]
            tail = jnp.exp(last - gcol[n])
            ends = mm(knt, split(jnp.concatenate([tail, tail], axis=1) * wu))
            whole = jnp.exp(last) * eye - ends[:, :GDIM]
            map_ref[v] = whole
            mapt_ref[v] = whole.T
            add_ref[v] = ends[:, GDIM:]
            reads = now * qn - mm(split(upto[n] * cross), split(wu[:, :GDIM]))
            pull_ref[v] = mm(split(reads.T), split(head_cols(cot_ref, v)))


def gdn_chain(
    map_ref, mapt_ref, add_ref, pull_ref, mem_ref, grad_ref,
    mem_in, mem_out, grad_in, grad_out, mem_send, mem_recv, grad_send, grad_recv,
):
    n = lax.axis_size("ctx")
    me = lax.axis_index("ctx")
    head_at = lax.axis_index("head")
    heads = map_ref.shape[0]
    right, left = lax.rem(me + 1, n), lax.rem(me + n - 1, n)
    barrier = pltpu.get_barrier_semaphore()
    for neighbour in (left, right):
        pl.semaphore_signal(barrier, inc=1, device_id=(neighbour, head_at), device_id_type=MESH)
    pl.semaphore_wait(barrier, 2)

    def send(source, target, send_sem, recv_sem, head, to):
        return pltpu.make_async_remote_copy(
            src_ref=source.at[head],
            dst_ref=target.at[head],
            send_sem=send_sem.at[head],
            recv_sem=recv_sem.at[head],
            device_id=(to, head_at),
            device_id_type=MESH,
        )

    def advance(head):
        copy = send(mem_out, mem_in, mem_send, mem_recv, head, right)

        @pl.when(me == 0)
        def _():
            mem_in[head] = jnp.zeros((GDIM, GDIM), F32)

        @pl.when(me > 0)
        def _():
            copy.wait_recv()

        @pl.when(me < n - 1)
        def _():
            mem_out[head] = mm(split(map_ref[head]), split(mem_in[head])) + add_ref[head]
            copy.start()

    def retreat(head):
        copy = send(grad_out, grad_in, grad_send, grad_recv, head, left)

        @pl.when(me == n - 1)
        def _():
            grad_in[head] = jnp.zeros((GDIM, GDIM), F32)

        @pl.when(me < n - 1)
        def _():
            copy.wait_recv()

        @pl.when(me > 0)
        def _():
            grad_out[head] = mm(split(mapt_ref[head]), split(grad_in[head])) + pull_ref[head]
            copy.start()

    lag = jnp.clip((n - 1 - 2 * me) * 3, -heads, heads)
    mem_late, grad_late = jnp.maximum(-lag, 0), jnp.maximum(lag, 0)

    def turn(step, carry):
        mem_head, grad_head = step - mem_late, step - grad_late

        @pl.when((mem_head >= 0) & (mem_head < heads))
        def _():
            advance(mem_head)

        @pl.when((grad_head >= 0) & (grad_head < heads))
        def _():
            retreat(grad_head)

        return carry

    lax.fori_loop(0, 2 * heads, turn, 0)

    def drain(head, carry):
        @pl.when(me < n - 1)
        def _():
            send(mem_out, mem_in, mem_send, mem_recv, head, right).wait_send()

        @pl.when(me > 0)
        def _():
            send(grad_out, grad_in, grad_send, grad_recv, head, left).wait_send()

        return carry

    lax.fori_loop(0, heads, drain, 0)
    mem_ref[...] = mem_in[...]
    grad_ref[...] = grad_in[...]


def gdn_grads(
    q_ref, k_ref, v_ref, cot_ref, decay_ref, write_ref, rate_ref, scale_ref,
    inv_ref, wu_ref, gam_ref, beta_ref, mem_ref, grad_ref,
    dq_ref, dk_ref, dv_ref, ddecay_ref, dwrite_ref,
):
    size = q_ref.shape[0]
    key_heads = q_ref.shape[1] // GDIM
    value_heads = v_ref.shape[1] // GDIM
    ratio = value_heads // key_heads
    rows, cols = triangles(size)
    gam, beta = gam_ref[...], beta_ref[...]
    dgam_rows, dbeta_rows, ends = [], [], []
    for m in range(key_heads):
        heads = list(range(m * ratio, (m + 1) * ratio))
        qn, qscale = unit_rows(head_cols(q_ref, m))
        kn, kscale = unit_rows(head_cols(k_ref, m))
        qs, ks = split(qn), split(kn)
        gram, cross = mm(ks, ks, 1, 1), mm(qs, ks, 1, 1)
        gcol = [column_form(gam[v : v + 1, :], size) for v in heads]
        bcol = [column_form(beta[v : v + 1, :], size) for v in heads]
        lasts = [gam[v : v + 1, size - 1 : size] for v in heads]
        now = [jnp.exp(c) for c in gcol]
        tail = [jnp.exp(e - c) for e, c in zip(lasts, gcol)]
        upto = [
            jnp.where(rows >= cols, jnp.exp(jnp.minimum(c - gam[v : v + 1, :], 0.0)), 0.0)
            for c, v in zip(gcol, heads)
        ]
        strict = [jnp.where(rows > cols, u, 0.0) for u in upto]
        mem = [mem_ref[v] for v in heads]
        grad = [grad_ref[v] for v in heads]
        mems, grads = [split(x) for x in mem], [split(x) for x in grad]
        cots = [split(head_cols(cot_ref, v)) for v in heads]
        written = [
            wu_ref[v][:, GDIM:] - mm(split(wu_ref[v][:, :GDIM]), s) for v, s in zip(heads, mems)
        ]
        ws = [split(w) for w in written]
        dwritten = [
            mm(split((u * cross).T), c) + t * mm(ks, g)
            for u, c, t, g in zip(upto, cots, tail, grads)
        ]
        target = [mm(split(inv_ref[v].T), split(d)) for v, d in zip(heads, dwritten)]
        xs = [split(x) for x in target]
        dcross = [u * mm(c, w, 1, 1) for u, c, w in zip(upto, cots, ws)]
        dsys = [-s * mm(x, w, 1, 1) for s, x, w in zip(strict, xs, ws)]
        dgram = [b * d for b, d in zip(bcol, dsys)]
        zq = [e * mm(c, s, 1, 1) for e, c, s in zip(now, cots, mems)]
        zk = [-e * mm(x, s, 1, 1) for e, x, s in zip(now, xs, mems)]
        wg = [t * mm(w, g, 1, 1) for t, w, g in zip(tail, ws, grads)]
        dqn, dkn = None, None
        cross_sum, gram_sum = dcross[0], dgram[0]
        dqn, dkn = zq[0], bcol[0] * zk[0] + wg[0]
        for n in range(1, ratio):
            cross_sum, gram_sum = cross_sum + dcross[n], gram_sum + dgram[n]
            dqn, dkn = dqn + zq[n], dkn + bcol[n] * zk[n] + wg[n]
        dqn = dqn + mm(split(cross_sum), ks)
        dkn = dkn + mm(split(cross_sum.T), qs) + mm(split(gram_sum + gram_sum.T), ks)
        for raw, scale, dn, out in ((qn, qscale, dqn, dq_ref), (kn, kscale, dkn, dk_ref)):
            along = jnp.sum(raw * dn, axis=-1, keepdims=True)
            out[:, m * GDIM : (m + 1) * GDIM] = scale * (dn - raw * along)
        for n, v in enumerate(heads):
            dv_ref[:, v * GDIM : (v + 1) * GDIM] = bcol[n] * target[n]
            pairs = dcross[n] * cross + dgram[n] * gram
            kept = kn * wg[n]
            old = kn * zk[n]
            by_row = pairs + qn * zq[n] + bcol[n] * old - kept
            dgam_rows.append(jnp.sum(by_row.T - pairs, axis=0, keepdims=True))
            values = head_cols(v_ref, v).astype(F32)
            by_beta = dsys[n] * gram + target[n] * values + old
            dbeta_rows.append(jnp.sum(by_beta.T, axis=0, keepdims=True))
            both = kept + jnp.exp(lasts[n]) * (mem[n] * grad[n])
            ends.append(jnp.sum(jnp.sum(both, axis=0, keepdims=True), axis=1, keepdims=True))
    dlog = lane_cumsum(jnp.concatenate(dgam_rows, axis=0), True) + jnp.concatenate(ends, axis=0)
    dbeta = jnp.concatenate(dbeta_rows, axis=0)
    ddecay_ref[...] = -rate_ref[...] * sigmoid(decay_ref[...]) * dlog
    gate = sigmoid(write_ref[...])
    dwrite_ref[...] = scale_ref[...] * gate * (1.0 - gate) * dbeta


def attention(lists_ref, q_ref, cot_ref, lse_ref, delta_ref, k_ref, v_ref, dq_ref, dkv_ref):
    score_scale = HD ** (-0.5)
    step = pl.program_id(0)
    tokens = q_ref.shape[0]
    heads = q_ref.shape[1] // HD
    keys = k_ref.shape[0]
    blocks_here = tokens // BLK
    n_blocks = lists_ref.shape[0] // (heads * TOPK)
    first = lax.axis_index("ctx") * blocks_here

    def stacked(ref):
        return jnp.concatenate([ref[:, h * HD : (h + 1) * HD] for h in range(heads)], axis=0)

    q, cot = stacked(q_ref), stacked(cot_ref)
    k, v = k_ref[...], v_ref[...]
    key_pos = step * keys + lax.broadcasted_iota(jnp.int32, (keys, tokens), 0)
    key_block = key_pos // BLK
    lane = lax.broadcasted_iota(jnp.int32, (1, tokens), 1)
    row_pos = first * BLK + lane
    row_block = row_pos // BLK
    own = (key_block == row_block) & (key_pos <= row_pos)
    before = key_block < row_block
    allowed = []
    for h in range(heads):
        member = None
        for t in range(TOPK):
            entry = jnp.zeros((1, tokens), jnp.int32)
            for b in range(blocks_here):
                listed = lists_ref[(h * n_blocks + first + b) * TOPK + t]
                entry = jnp.where(lane // BLK == b, listed, entry)
            hit = key_block == entry
            member = hit if member is None else member | hit
        allowed.append(own | (before & member))
    scores = mm((k, None), (q, None), 1, 1)
    dprobs = mm((v, None), (cot, None), 1, 1)
    probs, dscores = [], []
    for h in range(heads):
        span = slice(h * tokens, (h + 1) * tokens)
        mine = pl.ds(pl.multiple_of(first * BLK, tokens), tokens)
        lse, delta = lse_ref[h : h + 1, mine], delta_ref[h : h + 1, mine]
        prob = jnp.where(allowed[h], jnp.exp(scores[:, span] * score_scale - lse), 0.0)
        probs.append(prob)
        dscores.append(prob * (dprobs[:, span] - delta) * score_scale)
    ds = split(jnp.concatenate(dscores, axis=1))
    dkv_ref[:, :HD] = mm(ds, (q, None))
    dkv_ref[:, HD:] = mm(split(jnp.concatenate(probs, axis=1)), (cot, None))
    dq = mm(ds, (k, None), 0, 0)

    @pl.when(step == 0)
    def _():
        dq_ref[...] = jnp.zeros_like(dq_ref)

    for h in range(heads):
        dq_ref[:, h * HD : (h + 1) * HD] += dq[h * tokens : (h + 1) * tokens]


def on_device(
    attn_q, attn_k, attn_v, attn_cot, attn_lse, attn_delta, block_lists,
    gdn_q, gdn_k, gdn_v, decay_logit, write_logit, decay_rate, write_scale, gdn_cot,
):
    tokens = attn_q.shape[0]
    local_heads = attn_q.shape[1] // HD
    ctx = lax.axis_size("ctx")
    head_devices = lax.axis_size("head")
    n_rows = tokens * ctx
    kv_group = lax.axis_index("head") * local_heads // (Q_HEADS // KV_HEADS)
    own_kv = jnp.concatenate(
        [
            lax.dynamic_slice_in_dim(attn_k, kv_group * HD, HD, 1),
            lax.dynamic_slice_in_dim(attn_v, kv_group * HD, HD, 1),
        ],
        axis=1,
    )
    all_kv = lax.all_gather(own_kv, "ctx", axis=0, tiled=True)

    value_heads = gdn_v.shape[1] // GDIM
    rates, scales = decay_rate[:, None], write_scale[:, None]
    vmem = pl.BlockSpec(memory_space=pltpu.VMEM)
    square = jax.ShapeDtypeStruct((value_heads, GDIM, GDIM), F32)
    gates = jax.ShapeDtypeStruct((value_heads, tokens), F32)
    inverse, wu, maps, maps_t, adds, pulls, gam, beta = pl.pallas_call(
        gdn_local,
        out_shape=(
            jax.ShapeDtypeStruct((value_heads, tokens, tokens), F32),
            jax.ShapeDtypeStruct((value_heads, tokens, 2 * GDIM), F32),
            square, square, square, square, gates, gates,
        ),
        in_specs=[vmem] * 8,
        out_specs=[vmem] * 8,
        compiler_params=pltpu.CompilerParams(vmem_limit_bytes=VMEM_BYTES),
        name="gdn_local",
    )(gdn_q, gdn_k, gdn_v, gdn_cot, decay_logit, write_logit, rates, scales)

    keys = min(256, n_rows)
    grad_q, dkv = pl.pallas_call(
        attention,
        grid=(n_rows // keys,),
        out_shape=(
            jax.ShapeDtypeStruct((tokens, local_heads * HD), F32),
            jax.ShapeDtypeStruct((n_rows, 2 * HD), F32),
        ),
        in_specs=[
            pl.BlockSpec(memory_space=pltpu.SMEM),
            vmem, vmem, vmem, vmem,
            pl.BlockSpec((keys, HD), lambda i: (i, 0)),
            pl.BlockSpec((keys, HD), lambda i: (i, 1)),
        ],
        out_specs=(
            pl.BlockSpec((tokens, local_heads * HD), lambda i: (0, 0)),
            pl.BlockSpec((keys, 2 * HD), lambda i: (i, 0)),
        ),
        compiler_params=pltpu.CompilerParams(vmem_limit_bytes=VMEM_BYTES),
        name="attention",
    )(block_lists.reshape(-1), attn_q, attn_cot, attn_lse, attn_delta, all_kv, all_kv)

    mine = lax.psum_scatter(dkv, "ctx", scatter_dimension=0, tiled=True)
    groups = lax.all_gather(mine, "head", axis=0)
    groups = groups.reshape(KV_HEADS, head_devices // KV_HEADS, tokens, 2 * HD).sum(axis=1)
    attn_dk = jnp.concatenate([groups[c, :, :HD] for c in range(KV_HEADS)], axis=1)
    attn_dv = jnp.concatenate([groups[c, :, HD:] for c in range(KV_HEADS)], axis=1)

    buffer = pltpu.VMEM((value_heads, GDIM, GDIM), F32)
    sems = pltpu.SemaphoreType.DMA((value_heads,))
    mem, grad = pl.pallas_call(
        gdn_chain,
        out_shape=(square, square),
        in_specs=[vmem] * 4,
        out_specs=(vmem, vmem),
        scratch_shapes=[buffer] * 4 + [sems] * 4,
        compiler_params=pltpu.CompilerParams(
            collective_id=0, has_side_effects=True, vmem_limit_bytes=VMEM_BYTES
        ),
        name="gdn_chain",
    )(maps, maps_t, adds, pulls)

    dq, dk, dv, ddecay, dwrite = pl.pallas_call(
        gdn_grads,
        out_shape=(
            jax.ShapeDtypeStruct(gdn_q.shape, F32),
            jax.ShapeDtypeStruct(gdn_k.shape, F32),
            jax.ShapeDtypeStruct(gdn_v.shape, F32),
            gates, gates,
        ),
        in_specs=[vmem] * 14,
        out_specs=[vmem] * 5,
        compiler_params=pltpu.CompilerParams(vmem_limit_bytes=VMEM_BYTES),
        name="gdn_grads",
    )(
        gdn_q, gdn_k, gdn_v, gdn_cot, decay_logit, write_logit, rates, scales,
        inverse, wu, gam, beta, mem, grad,
    )
    return (grad_q, attn_dk, attn_dv, dq, dk, dv, ddecay, dwrite)


def solution(mesh):
    return jax.shard_map(
        on_device,
        mesh=mesh,
        in_specs=(
            P("ctx", "head"), P("ctx", None), P("ctx", None), P("ctx", "head"),
            P("head", None), P("head", None), P("head", None, None),
            P("ctx", "head"), P("ctx", "head"), P("ctx", "head"),
            P("head", "ctx"), P("head", "ctx"), P("head"), P("head"), P("ctx", "head"),
        ),
        out_specs=(
            P("ctx", "head"), P("ctx", None), P("ctx", None),
            P("ctx", "head"), P("ctx", "head"), P("ctx", "head"),
            P("head", "ctx"), P("head", "ctx"),
        ),
        check_vma=False,
    )
```

```python
import jax
import jax.numpy as jnp
from jax import lax
from jax.experimental import pallas as pl
from jax.experimental.pallas import tpu as pltpu
from jax.sharding import PartitionSpec as P

Q_HEADS = 16
KV_HEADS = 2
HD = 256
GDIM = 128
BLK = 64
TOPK = 4
F32 = jnp.float32
BF16 = jnp.bfloat16
VMEM_BYTES = 48 * 1024 * 1024
MESH = pl.DeviceIdType.MESH


def split(x):
    if x.dtype == BF16:
        return (x, None)
    head = x.astype(BF16)
    return (head, (x - head.astype(F32)).astype(BF16))


def mm(a, b, ca=1, cb=0):
    dims = (((ca,), (cb,)), ((), ()))
    out = lax.dot_general(a[0], b[0], dims, preferred_element_type=F32)
    if b[1] is not None:
        out = out + lax.dot_general(a[0], b[1], dims, preferred_element_type=F32)
    if a[1] is not None:
        out = out + lax.dot_general(a[1], b[0], dims, preferred_element_type=F32)
    return out


def lane_cumsum(x, backward):
    width = x.shape[1]
    lanes = lax.broadcasted_iota(jnp.int32, x.shape, 1)
    step = 1
    while step < width:
        moved = pltpu.roll(x, width - step if backward else step, 1)
        keep = lanes < width - step if backward else lanes >= step
        x = x + jnp.where(keep, moved, 0.0)
        step *= 2
    return x


def softplus(x):
    return jnp.maximum(x, 0.0) + jnp.log(1.0 + jnp.exp(-jnp.abs(x)))


def sigmoid(x):
    return 1.0 / (1.0 + jnp.exp(-x))


def column_form(row, size):
    return jnp.broadcast_to(row, (size, size)).T


def unit_rows(raw):
    full = raw.astype(F32)
    scale = lax.rsqrt(jnp.sum(full * full, axis=-1, keepdims=True) + 1e-06)
    return full * scale, scale


def head_cols(ref, head):
    return ref[:, head * GDIM : (head + 1) * GDIM]


def triangles(size):
    rows = lax.broadcasted_iota(jnp.int32, (size, size), 0)
    cols = lax.broadcasted_iota(jnp.int32, (size, size), 1)
    return rows, cols


def gdn_local(
    q_ref, k_ref, v_ref, cot_ref, decay_ref, write_ref, rate_ref, scale_ref,
    inv_ref, wu_ref, map_ref, mapt_ref, add_ref, pull_ref, gam_ref, beta_ref,
):
    size = q_ref.shape[0]
    key_heads = q_ref.shape[1] // GDIM
    value_heads = v_ref.shape[1] // GDIM
    ratio = value_heads // key_heads
    gam = lane_cumsum(-rate_ref[...] * softplus(decay_ref[...]), False)
    beta = scale_ref[...] * sigmoid(write_ref[...])
    gam_ref[...] = gam
    beta_ref[...] = beta
    rows, cols = triangles(size)
    eye = jnp.where(rows == cols, 1.0, 0.0)
    group = min(4, value_heads)
    for first in range(0, value_heads, group):
        heads = list(range(first, first + group))
        keyed = {}
        for m in sorted({v // ratio for v in heads}):
            qn, kn = unit_rows(head_cols(q_ref, m))[0], unit_rows(head_cols(k_ref, m))[0]
            qs, ks = split(qn), split(kn)
            keyed[m] = (qn, kn, mm(ks, ks, 1, 1), mm(qs, ks, 1, 1), split(kn.T))
        gcol = [column_form(gam[v : v + 1, :], size) for v in heads]
        bcol = [column_form(beta[v : v + 1, :], size) for v in heads]
        upto = [
            jnp.where(rows >= cols, jnp.exp(jnp.minimum(c - gam[v : v + 1, :], 0.0)), 0.0)
            for c, v in zip(gcol, heads)
        ]
        system = [
            jnp.where(rows > cols, b * u * keyed[v // ratio][2], 0.0)
            for b, u, v in zip(bcol, upto, heads)
        ]
        inverse = [eye - jnp.where(rows // 2 == cols // 2, s, 0.0) for s in system]
        half = 2
        while half < size:
            low = (rows // half == cols // half + 1) & ((rows // half) % 2 == 1)
            parts = [split(t) for t in inverse]
            inner = [mm(split(jnp.where(low, s, 0.0)), t) for s, t in zip(system, parts)]
            outer = [mm(t, split(x)) for t, x in zip(parts, inner)]
            inverse = [t - x for t, x in zip(inverse, outer)]
            half *= 2
        for n, v in enumerate(heads):
            qn, kn, gram, cross, knt = keyed[v // ratio]
            now = jnp.exp(gcol[n])
            inv_ref[v] = inverse[n]
            targets = jnp.concatenate(
                [bcol[n] * now * kn, bcol[n] * head_cols(v_ref, v).astype(F32)], axis=1
            )
            wu = mm(split(inverse[n]), split(targets))
            wu_ref[v] = wu
            last = gam[v : v + 1, size - 1 : size]
            tail = jnp.exp(last - gcol[n])
            ends = mm(knt, split(jnp.concatenate([tail, tail], axis=1) * wu))
            whole = jnp.exp(last) * eye - ends[:, :GDIM]
            map_ref[v] = whole
            mapt_ref[v] = whole.T
            add_ref[v] = ends[:, GDIM:]
            reads = now * qn - mm(split(upto[n] * cross), split(wu[:, :GDIM]))
            pull_ref[v] = mm(split(reads.T), split(head_cols(cot_ref, v)))


def gdn_chain(
    map_ref, mapt_ref, add_ref, pull_ref, dkv_ref, mem_ref, grad_ref, adk_ref, adv_ref,
    mem_in, mem_out, grad_in, grad_out, sums, groups,
    mem_send, mem_recv, grad_send, grad_recv, sum_send, sum_recv, group_send, group_recv,
):
    n = lax.axis_size("ctx")
    me = lax.axis_index("ctx")
    head_at = lax.axis_index("head")
    heads = map_ref.shape[0]
    right, left = lax.rem(me + 1, n), lax.rem(me + n - 1, n)
    barrier = pltpu.get_barrier_semaphore()
    for neighbour in (left, right):
        pl.semaphore_signal(barrier, inc=1, device_id=(neighbour, head_at), device_id_type=MESH)
    others = lax.axis_size("head")
    for d in range(1, others):
        pl.semaphore_signal(
            barrier, inc=1, device_id=(me, lax.rem(head_at + d, others)), device_id_type=MESH
        )
    pl.semaphore_wait(barrier, 1 + others)

    def send(source, target, send_sem, recv_sem, head, to):
        return pltpu.make_async_remote_copy(
            src_ref=source.at[head],
            dst_ref=target.at[head],
            send_sem=send_sem.at[head],
            recv_sem=recv_sem.at[head],
            device_id=(to, head_at),
            device_id_type=MESH,
        )

    def advance(head):
        copy = send(mem_out, mem_in, mem_send, mem_recv, head, right)

        @pl.when(me == 0)
        def _():
            mem_in[head] = jnp.zeros((GDIM, GDIM), F32)

        @pl.when(me > 0)
        def _():
            copy.wait_recv()

        @pl.when(me < n - 1)
        def _():
            mem_out[head] = mm(split(map_ref[head]), split(mem_in[head])) + add_ref[head]
            copy.start()

    def retreat(head):
        copy = send(grad_out, grad_in, grad_send, grad_recv, head, left)

        @pl.when(me == n - 1)
        def _():
            grad_in[head] = jnp.zeros((GDIM, GDIM), F32)

        @pl.when(me < n - 1)
        def _():
            copy.wait_recv()

        @pl.when(me > 0)
        def _():
            grad_out[head] = mm(split(mapt_ref[head]), split(grad_in[head])) + pull_ref[head]
            copy.start()

    def share(d):
        return pltpu.make_async_remote_copy(
            src_ref=groups.at[head_at],
            dst_ref=groups.at[head_at],
            send_sem=group_send.at[d],
            recv_sem=group_recv.at[d],
            device_id=(me, lax.rem(head_at + d, others)),
            device_id_type=MESH,
        )

    def gather_sum(owner):
        copy = send(sums, sums, sum_send, sum_recv, owner, left)

        @pl.when(me == n - 1)
        def _():
            sums[owner] = dkv_ref[owner]

        @pl.when(me < n - 1)
        def _():
            copy.wait_recv()
            sums[owner] = sums[owner] + dkv_ref[owner]

        @pl.when(owner < me)
        def _():
            copy.start()

        @pl.when(owner == me)
        def _():
            groups[head_at] = sums[owner]
            for d in range(1, others):
                share(d).start()

    lag = jnp.clip((n - 1 - 2 * me) * 3, -heads, heads)
    mem_late, grad_late = jnp.maximum(-lag, 0), jnp.maximum(lag, 0)

    def turn(step, carry):
        mem_head, grad_head = step - mem_late, step - grad_late

        @pl.when((mem_head >= 0) & (mem_head < heads))
        def _():
            advance(mem_head)

        @pl.when((grad_head >= 0) & (grad_head < heads))
        def _():
            retreat(grad_head)

        sum_step = step - (n - 1 - me)
        owner = lax.div(sum_step, 2)

        @pl.when((sum_step >= 0) & (lax.rem(sum_step, 2) == 0) & (owner <= me))
        def _():
            gather_sum(owner)

        return carry

    lax.fori_loop(0, max(2 * heads, 3 * n), turn, 0)

    def drain(head, carry):
        @pl.when(me < n - 1)
        def _():
            send(mem_out, mem_in, mem_send, mem_recv, head, right).wait_send()

        @pl.when(me > 0)
        def _():
            send(grad_out, grad_in, grad_send, grad_recv, head, left).wait_send()

        return carry

    lax.fori_loop(0, heads, drain, 0)

    def drain_sums(owner, carry):
        @pl.when(owner < me)
        def _():
            send(sums, sums, sum_send, sum_recv, owner, left).wait_send()

        return carry

    lax.fori_loop(0, n, drain_sums, 0)
    for d in range(1, others):
        here = lax.rem(head_at + others - d, others)
        pltpu.make_async_remote_copy(
            src_ref=groups.at[here],
            dst_ref=groups.at[here],
            send_sem=group_send.at[d],
            recv_sem=group_recv.at[d],
            device_id=(me, here),
            device_id_type=MESH,
        ).wait_recv()
    each = others // KV_HEADS
    for c in range(KV_HEADS):
        total = groups[c * each]
        for d in range(1, each):
            total = total + groups[c * each + d]
        adk_ref[:, c * HD : (c + 1) * HD] = total[:, :HD]
        adv_ref[:, c * HD : (c + 1) * HD] = total[:, HD:]
    for d in range(1, others):
        share(d).wait_send()
    mem_ref[...] = mem_in[...]
    grad_ref[...] = grad_in[...]


def gdn_grads(
    q_ref, k_ref, v_ref, cot_ref, decay_ref, write_ref, rate_ref, scale_ref,
    inv_ref, wu_ref, gam_ref, beta_ref, mem_ref, grad_ref,
    dq_ref, dk_ref, dv_ref, ddecay_ref, dwrite_ref,
):
    size = q_ref.shape[0]
    key_heads = q_ref.shape[1] // GDIM
    value_heads = v_ref.shape[1] // GDIM
    ratio = value_heads // key_heads
    rows, cols = triangles(size)
    gam, beta = gam_ref[...], beta_ref[...]
    dgam_rows, dbeta_rows, ends = [], [], []
    for m in range(key_heads):
        heads = list(range(m * ratio, (m + 1) * ratio))
        qn, qscale = unit_rows(head_cols(q_ref, m))
        kn, kscale = unit_rows(head_cols(k_ref, m))
        qs, ks = split(qn), split(kn)
        gram, cross = mm(ks, ks, 1, 1), mm(qs, ks, 1, 1)
        gcol = [column_form(gam[v : v + 1, :], size) for v in heads]
        bcol = [column_form(beta[v : v + 1, :], size) for v in heads]
        lasts = [gam[v : v + 1, size - 1 : size] for v in heads]
        now = [jnp.exp(c) for c in gcol]
        tail = [jnp.exp(e - c) for e, c in zip(lasts, gcol)]
        upto = [
            jnp.where(rows >= cols, jnp.exp(jnp.minimum(c - gam[v : v + 1, :], 0.0)), 0.0)
            for c, v in zip(gcol, heads)
        ]
        strict = [jnp.where(rows > cols, u, 0.0) for u in upto]
        mem = [mem_ref[v] for v in heads]
        grad = [grad_ref[v] for v in heads]
        mems, grads = [split(x) for x in mem], [split(x) for x in grad]
        cots = [split(head_cols(cot_ref, v)) for v in heads]
        written = [
            wu_ref[v][:, GDIM:] - mm(split(wu_ref[v][:, :GDIM]), s) for v, s in zip(heads, mems)
        ]
        ws = [split(w) for w in written]
        dwritten = [
            mm(split((u * cross).T), c) + t * mm(ks, g)
            for u, c, t, g in zip(upto, cots, tail, grads)
        ]
        target = [mm(split(inv_ref[v].T), split(d)) for v, d in zip(heads, dwritten)]
        xs = [split(x) for x in target]
        dcross = [u * mm(c, w, 1, 1) for u, c, w in zip(upto, cots, ws)]
        dsys = [-s * mm(x, w, 1, 1) for s, x, w in zip(strict, xs, ws)]
        dgram = [b * d for b, d in zip(bcol, dsys)]
        zq = [e * mm(c, s, 1, 1) for e, c, s in zip(now, cots, mems)]
        zk = [-e * mm(x, s, 1, 1) for e, x, s in zip(now, xs, mems)]
        wg = [t * mm(w, g, 1, 1) for t, w, g in zip(tail, ws, grads)]
        dqn, dkn = None, None
        cross_sum, gram_sum = dcross[0], dgram[0]
        dqn, dkn = zq[0], bcol[0] * zk[0] + wg[0]
        for n in range(1, ratio):
            cross_sum, gram_sum = cross_sum + dcross[n], gram_sum + dgram[n]
            dqn, dkn = dqn + zq[n], dkn + bcol[n] * zk[n] + wg[n]
        dqn = dqn + mm(split(cross_sum), ks)
        dkn = dkn + mm(split(cross_sum.T), qs) + mm(split(gram_sum + gram_sum.T), ks)
        for raw, scale, dn, out in ((qn, qscale, dqn, dq_ref), (kn, kscale, dkn, dk_ref)):
            along = jnp.sum(raw * dn, axis=-1, keepdims=True)
            out[:, m * GDIM : (m + 1) * GDIM] = scale * (dn - raw * along)
        for n, v in enumerate(heads):
            dv_ref[:, v * GDIM : (v + 1) * GDIM] = bcol[n] * target[n]
            pairs = dcross[n] * cross + dgram[n] * gram
            kept = kn * wg[n]
            old = kn * zk[n]
            by_row = pairs + qn * zq[n] + bcol[n] * old - kept
            dgam_rows.append(jnp.sum(by_row.T - pairs, axis=0, keepdims=True))
            values = head_cols(v_ref, v).astype(F32)
            by_beta = dsys[n] * gram + target[n] * values + old
            dbeta_rows.append(jnp.sum(by_beta.T, axis=0, keepdims=True))
            both = kept + jnp.exp(lasts[n]) * (mem[n] * grad[n])
            ends.append(jnp.sum(jnp.sum(both, axis=0, keepdims=True), axis=1, keepdims=True))
    dlog = lane_cumsum(jnp.concatenate(dgam_rows, axis=0), True) + jnp.concatenate(ends, axis=0)
    dbeta = jnp.concatenate(dbeta_rows, axis=0)
    ddecay_ref[...] = -rate_ref[...] * sigmoid(decay_ref[...]) * dlog
    gate = sigmoid(write_ref[...])
    dwrite_ref[...] = scale_ref[...] * gate * (1.0 - gate) * dbeta


def attention(lists_ref, q_ref, cot_ref, lse_ref, delta_ref, kv_ref, dq_ref, dkv_ref, q_all, cot_all):
    score_scale = HD ** (-0.5)
    me = lax.axis_index("ctx")
    tokens = q_ref.shape[0]
    heads = q_ref.shape[1] // HD
    blocks_here = tokens // BLK
    n_blocks = lists_ref.shape[0] // (heads * TOPK)
    first = me * blocks_here
    for h in range(heads):
        q_all[h * tokens : (h + 1) * tokens, :] = q_ref[:, h * HD : (h + 1) * HD]
        cot_all[h * tokens : (h + 1) * tokens, :] = cot_ref[:, h * HD : (h + 1) * HD]
    dq_ref[...] = jnp.zeros_like(dq_ref)
    lane = lax.broadcasted_iota(jnp.int32, (1, tokens), 1)
    row_pos = me * tokens + lane
    row_block = row_pos // BLK
    mine = pl.ds(pl.multiple_of(me * tokens, tokens), tokens)

    def block(owner):
        q, cot = (q_all[...], None), (cot_all[...], None)
        k, v = (kv_ref[owner][:, :HD], None), (kv_ref[owner][:, HD:], None)
        key_pos = owner * tokens + lax.broadcasted_iota(jnp.int32, (tokens, tokens), 0)
        key_block = key_pos // BLK
        own = (key_block == row_block) & (key_pos <= row_pos)
        before = key_block < row_block
        scores = mm(k, q, 1, 1)
        dprobs = mm(v, cot, 1, 1)
        probs, dscores = [], []
        for h in range(heads):
            member = None
            for t in range(TOPK):
                entry = jnp.zeros((1, tokens), jnp.int32)
                for b in range(blocks_here):
                    listed = lists_ref[(h * n_blocks + first + b) * TOPK + t]
                    entry = jnp.where(lane // BLK == b, listed, entry)
                hit = key_block == entry
                member = hit if member is None else member | hit
            allowed = own | (before & member)
            span = slice(h * tokens, (h + 1) * tokens)
            lse, delta = lse_ref[h : h + 1, mine], delta_ref[h : h + 1, mine]
            prob = jnp.where(allowed, jnp.exp(scores[:, span] * score_scale - lse), 0.0)
            probs.append(prob)
            dscores.append(prob * (dprobs[:, span] - delta) * score_scale)
        ds = split(jnp.concatenate(dscores, axis=1))
        dkv_ref[owner, :, :HD] = mm(ds, q)
        dkv_ref[owner, :, HD:] = mm(split(jnp.concatenate(probs, axis=1)), cot)
        dq = mm(ds, k, 0, 0)
        for h in range(heads):
            dq_ref[:, h * HD : (h + 1) * HD] += dq[h * tokens : (h + 1) * tokens]

    return block


def local_part(
    lists_ref, aq_ref, acot_ref, lse_ref, delta_ref, ak_ref, av_ref,
    q_ref, k_ref, v_ref, cot_ref, decay_ref, write_ref, rate_ref, scale_ref,
    inv_ref, wu_ref, map_ref, mapt_ref, add_ref, pull_ref, gam_ref, beta_ref, dq_ref, dkv_ref,
    kv, q_all, cot_all, far_send, far_recv, near_send, near_recv,
):
    n = lax.axis_size("ctx")
    me, head_at = lax.axis_index("ctx"), lax.axis_index("head")
    heads = aq_ref.shape[1] // HD
    chips = n // 2
    twin = me + 1 - 2 * lax.rem(me, 2)
    barrier = pltpu.get_barrier_semaphore()
    for d in range(1, n):
        pl.semaphore_signal(
            barrier, inc=1, device_id=(lax.rem(me + d, n), head_at), device_id_type=MESH
        )
    pl.semaphore_wait(barrier, n - 1)

    group = head_at * heads // (Q_HEADS // KV_HEADS)
    columns = pl.ds(pl.multiple_of(group * HD, HD), HD)
    kv[me, :, :HD] = ak_ref[:, columns]
    kv[me, :, HD:] = av_ref[:, columns]

    def copy(slot, send_sem, recv_sem, index, to):
        return pltpu.make_async_remote_copy(
            src_ref=kv.at[slot],
            dst_ref=kv.at[slot],
            send_sem=send_sem.at[index],
            recv_sem=recv_sem.at[index],
            device_id=(to, head_at),
            device_id_type=MESH,
        )

    def source(d):
        return lax.rem(me + n - 2 * d, n)

    def far(d):
        return copy(me, far_send, far_recv, d, lax.rem(me + 2 * d, n))

    for d in range(1, chips):
        far(d).start()
    copy(me, near_send, near_recv, 0, twin).start()

    gdn_local(
        q_ref, k_ref, v_ref, cot_ref, decay_ref, write_ref, rate_ref, scale_ref,
        inv_ref, wu_ref, map_ref, mapt_ref, add_ref, pull_ref, gam_ref, beta_ref,
    )
    block = attention(
        lists_ref, aq_ref, acot_ref, lse_ref, delta_ref, kv, dq_ref, dkv_ref, q_all, cot_all
    )
    for d in range(1, chips):
        copy(source(d), far_send, far_recv, d, twin).wait_recv()
        copy(source(d), near_send, near_recv, d, twin).start()

    def visit(start):
        def turn(d, carry):
            owner = lax.rem(start + n - 2 * d, n)

            @pl.when(owner <= me)
            def _():
                block(owner)

            return carry

        lax.fori_loop(0, chips, turn, 0)

    visit(me)
    for d in range(chips):
        copy(lax.rem(twin + n - 2 * d, n), near_send, near_recv, d, twin).wait_recv()
    visit(twin)
    for d in range(1, chips):
        far(d).wait_send()
    for d in range(chips):
        copy(source(d), near_send, near_recv, d, twin).wait_send()


def on_device(
    attn_q, attn_k, attn_v, attn_cot, attn_lse, attn_delta, block_lists,
    gdn_q, gdn_k, gdn_v, decay_logit, write_logit, decay_rate, write_scale, gdn_cot,
):
    tokens = attn_q.shape[0]
    local_heads = attn_q.shape[1] // HD
    ctx = lax.axis_size("ctx")
    head_devices = lax.axis_size("head")
    value_heads = gdn_v.shape[1] // GDIM
    rates, scales = decay_rate[:, None], write_scale[:, None]
    vmem = pl.BlockSpec(memory_space=pltpu.VMEM)
    square = jax.ShapeDtypeStruct((value_heads, GDIM, GDIM), F32)
    gates = jax.ShapeDtypeStruct((value_heads, tokens), F32)
    sums = (ctx, tokens, 2 * HD)
    far, near = pltpu.SemaphoreType.DMA((ctx // 2,)), pltpu.SemaphoreType.DMA((ctx // 2,))
    inverse, wu, maps, maps_t, adds, pulls, gam, beta, grad_q, dkv = pl.pallas_call(
        local_part,
        out_shape=(
            jax.ShapeDtypeStruct((value_heads, tokens, tokens), F32),
            jax.ShapeDtypeStruct((value_heads, tokens, 2 * GDIM), F32),
            square, square, square, square, gates, gates,
            jax.ShapeDtypeStruct((tokens, local_heads * HD), F32),
            jax.ShapeDtypeStruct(sums, F32),
        ),
        in_specs=[pl.BlockSpec(memory_space=pltpu.SMEM)] + [vmem] * 14,
        out_specs=[vmem] * 10,
        scratch_shapes=[
            pltpu.VMEM(sums, BF16),
            pltpu.VMEM((local_heads * tokens, HD), BF16),
            pltpu.VMEM((local_heads * tokens, HD), BF16),
            far, far, near, near,
        ],
        compiler_params=pltpu.CompilerParams(
            collective_id=0, has_side_effects=True, vmem_limit_bytes=VMEM_BYTES
        ),
        name="local_part",
    )(
        block_lists.reshape(-1), attn_q, attn_cot, attn_lse, attn_delta, attn_k, attn_v,
        gdn_q, gdn_k, gdn_v, gdn_cot, decay_logit, write_logit, rates, scales,
    )

    buffer = pltpu.VMEM((value_heads, GDIM, GDIM), F32)
    sems = pltpu.SemaphoreType.DMA((value_heads,))
    sum_sems = pltpu.SemaphoreType.DMA((ctx,))
    head_sems = pltpu.SemaphoreType.DMA((head_devices,))
    key_grads = jax.ShapeDtypeStruct((tokens, KV_HEADS * HD), F32)
    mem, grad, attn_dk, attn_dv = pl.pallas_call(
        gdn_chain,
        out_shape=(square, square, key_grads, key_grads),
        in_specs=[vmem] * 5,
        out_specs=[vmem] * 4,
        scratch_shapes=[buffer] * 4
        + [pltpu.VMEM(sums, F32), pltpu.VMEM((head_devices, tokens, 2 * HD), F32)]
        + [sems] * 4
        + [sum_sems] * 2
        + [head_sems] * 2,
        compiler_params=pltpu.CompilerParams(
            collective_id=1, has_side_effects=True, vmem_limit_bytes=VMEM_BYTES
        ),
        name="gdn_chain",
    )(maps, maps_t, adds, pulls, dkv)

    dq, dk, dv, ddecay, dwrite = pl.pallas_call(
        gdn_grads,
        out_shape=(
            jax.ShapeDtypeStruct(gdn_q.shape, F32),
            jax.ShapeDtypeStruct(gdn_k.shape, F32),
            jax.ShapeDtypeStruct(gdn_v.shape, F32),
            gates, gates,
        ),
        in_specs=[vmem] * 14,
        out_specs=[vmem] * 5,
        compiler_params=pltpu.CompilerParams(vmem_limit_bytes=VMEM_BYTES),
        name="gdn_grads",
    )(
        gdn_q, gdn_k, gdn_v, gdn_cot, decay_logit, write_logit, rates, scales,
        inverse, wu, gam, beta, mem, grad,
    )
    return (grad_q, attn_dk, attn_dv, dq, dk, dv, ddecay, dwrite)


def solution(mesh):
    return jax.shard_map(
        on_device,
        mesh=mesh,
        in_specs=(
            P("ctx", "head"), P("ctx", None), P("ctx", None), P("ctx", "head"),
            P("head", None), P("head", None), P("head", None, None),
            P("ctx", "head"), P("ctx", "head"), P("ctx", "head"),
            P("head", "ctx"), P("head", "ctx"), P("head"), P("head"), P("ctx", "head"),
        ),
        out_specs=(
            P("ctx", "head"), P("ctx", None), P("ctx", None),
            P("ctx", "head"), P("ctx", "head"), P("ctx", "head"),
            P("head", "ctx"), P("head", "ctx"),
        ),
        check_vma=False,
    )
```

```python
import jax
import jax.numpy as jnp
from jax import lax
from jax.experimental import pallas as pl
from jax.experimental.pallas import tpu as pltpu
from jax.sharding import PartitionSpec as P

Q_HEADS = 16
KV_HEADS = 2
HD = 256
GDIM = 128
BLK = 64
TOPK = 4
F32 = jnp.float32
BF16 = jnp.bfloat16
VMEM_BYTES = 58 * 1024 * 1024
MESH = pl.DeviceIdType.MESH


def split(x):
    if x.dtype == BF16:
        return (x, None)
    head = x.astype(BF16)
    return (head, (x - head.astype(F32)).astype(BF16))


def mm(a, b, ca=1, cb=0):
    dims = (((ca,), (cb,)), ((), ()))
    out = lax.dot_general(a[0], b[0], dims, preferred_element_type=F32)
    if b[1] is not None:
        out = out + lax.dot_general(a[0], b[1], dims, preferred_element_type=F32)
    if a[1] is not None:
        out = out + lax.dot_general(a[1], b[0], dims, preferred_element_type=F32)
    return out


def lane_cumsum(x, backward):
    width = x.shape[1]
    lanes = lax.broadcasted_iota(jnp.int32, x.shape, 1)
    step = 1
    while step < width:
        moved = pltpu.roll(x, width - step if backward else step, 1)
        keep = lanes < width - step if backward else lanes >= step
        x = x + jnp.where(keep, moved, 0.0)
        step *= 2
    return x


def softplus(x):
    return jnp.maximum(x, 0.0) + jnp.log(1.0 + jnp.exp(-jnp.abs(x)))


def sigmoid(x):
    return 1.0 / (1.0 + jnp.exp(-x))


def column_form(row, size):
    return jnp.broadcast_to(row, (size, size)).T


def unit_rows(raw):
    full = raw.astype(F32)
    scale = lax.rsqrt(jnp.sum(full * full, axis=-1, keepdims=True) + 1e-06)
    return full * scale, scale


def head_cols(ref, head):
    return ref[:, head * GDIM : (head + 1) * GDIM]


def per_head(ref, like):
    heads, width = like.shape
    return jnp.concatenate([jnp.full((1, width), ref[v], F32) for v in range(heads)], axis=0)


def triangles(size):
    rows = lax.broadcasted_iota(jnp.int32, (size, size), 0)
    cols = lax.broadcasted_iota(jnp.int32, (size, size), 1)
    return rows, cols


def gdn_local(
    q_ref, k_ref, v_ref, cot_ref, decay_ref, write_ref, rate_ref, scale_ref,
    inv_ref, wu_ref, map_ref, mapt_ref, add_ref, pull_ref, gam_ref, beta_ref,
):
    size = q_ref.shape[0]
    key_heads = q_ref.shape[1] // GDIM
    value_heads = v_ref.shape[1] // GDIM
    ratio = value_heads // key_heads
    gam = lane_cumsum(-per_head(rate_ref, decay_ref) * softplus(decay_ref[...]), False)
    beta = per_head(scale_ref, write_ref) * sigmoid(write_ref[...])
    gam_ref[...] = gam
    beta_ref[...] = beta
    rows, cols = triangles(size)
    eye = jnp.where(rows == cols, 1.0, 0.0)
    group = min(4, value_heads)
    for first in range(0, value_heads, group):
        heads = list(range(first, first + group))
        keyed = {}
        for m in sorted({v // ratio for v in heads}):
            qn, kn = unit_rows(head_cols(q_ref, m))[0], unit_rows(head_cols(k_ref, m))[0]
            qs, ks = split(qn), split(kn)
            keyed[m] = (qn, kn, mm(ks, ks, 1, 1), mm(qs, ks, 1, 1), split(kn.T))
        gcol = [column_form(gam[v : v + 1, :], size) for v in heads]
        bcol = [column_form(beta[v : v + 1, :], size) for v in heads]
        upto = [
            jnp.where(rows >= cols, jnp.exp(jnp.minimum(c - gam[v : v + 1, :], 0.0)), 0.0)
            for c, v in zip(gcol, heads)
        ]
        system = [
            jnp.where(rows > cols, b * u * keyed[v // ratio][2], 0.0)
            for b, u, v in zip(bcol, upto, heads)
        ]
        inverse = [eye - jnp.where(rows // 2 == cols // 2, s, 0.0) for s in system]
        half = 2
        while half < size:
            low = (rows // half == cols // half + 1) & ((rows // half) % 2 == 1)
            parts = [split(t) for t in inverse]
            inner = [mm(split(jnp.where(low, s, 0.0)), t) for s, t in zip(system, parts)]
            outer = [mm(t, split(x)) for t, x in zip(parts, inner)]
            inverse = [t - x for t, x in zip(inverse, outer)]
            half *= 2
        for n, v in enumerate(heads):
            qn, kn, gram, cross, knt = keyed[v // ratio]
            now = jnp.exp(gcol[n])
            inv_ref[v] = inverse[n]
            targets = jnp.concatenate(
                [bcol[n] * now * kn, bcol[n] * head_cols(v_ref, v).astype(F32)], axis=1
            )
            wu = mm(split(inverse[n]), split(targets))
            wu_ref[v] = wu
            last = gam[v : v + 1, size - 1 : size]
            tail = jnp.exp(last - gcol[n])
            ends = mm(knt, split(jnp.concatenate([tail, tail], axis=1) * wu))
            whole = jnp.exp(last) * eye - ends[:, :GDIM]
            map_ref[v] = whole
            mapt_ref[v] = whole.T
            add_ref[v] = ends[:, GDIM:]
            reads = now * qn - mm(split(upto[n] * cross), split(wu[:, :GDIM]))
            pull_ref[v] = mm(split(reads.T), split(head_cols(cot_ref, v)))


def gdn_grads(
    q_ref, k_ref, v_ref, cot_ref, decay_ref, write_ref, rate_ref, scale_ref,
    inv_ref, wu_ref, gam_ref, beta_ref, mem_ref, grad_ref,
    dq_ref, dk_ref, dv_ref, ddecay_ref, dwrite_ref,
):
    size = q_ref.shape[0]
    key_heads = q_ref.shape[1] // GDIM
    value_heads = v_ref.shape[1] // GDIM
    ratio = value_heads // key_heads
    rows, cols = triangles(size)
    gam, beta = gam_ref[...], beta_ref[...]
    dgam_rows, dbeta_rows, ends = [], [], []
    for m in range(key_heads):
        heads = list(range(m * ratio, (m + 1) * ratio))
        qn, qscale = unit_rows(head_cols(q_ref, m))
        kn, kscale = unit_rows(head_cols(k_ref, m))
        qs, ks = split(qn), split(kn)
        gram, cross = mm(ks, ks, 1, 1), mm(qs, ks, 1, 1)
        gcol = [column_form(gam[v : v + 1, :], size) for v in heads]
        bcol = [column_form(beta[v : v + 1, :], size) for v in heads]
        lasts = [gam[v : v + 1, size - 1 : size] for v in heads]
        now = [jnp.exp(c) for c in gcol]
        tail = [jnp.exp(e - c) for e, c in zip(lasts, gcol)]
        upto = [
            jnp.where(rows >= cols, jnp.exp(jnp.minimum(c - gam[v : v + 1, :], 0.0)), 0.0)
            for c, v in zip(gcol, heads)
        ]
        strict = [jnp.where(rows > cols, u, 0.0) for u in upto]
        mem = [mem_ref[v] for v in heads]
        grad = [grad_ref[v] for v in heads]
        mems, grads = [split(x) for x in mem], [split(x) for x in grad]
        cots = [split(head_cols(cot_ref, v)) for v in heads]
        written = [
            wu_ref[v][:, GDIM:] - mm(split(wu_ref[v][:, :GDIM]), s) for v, s in zip(heads, mems)
        ]
        ws = [split(w) for w in written]
        dwritten = [
            mm(split((u * cross).T), c) + t * mm(ks, g)
            for u, c, t, g in zip(upto, cots, tail, grads)
        ]
        target = [mm(split(inv_ref[v].T), split(d)) for v, d in zip(heads, dwritten)]
        xs = [split(x) for x in target]
        dcross = [u * mm(c, w, 1, 1) for u, c, w in zip(upto, cots, ws)]
        dsys = [-s * mm(x, w, 1, 1) for s, x, w in zip(strict, xs, ws)]
        dgram = [b * d for b, d in zip(bcol, dsys)]
        zq = [e * mm(c, s, 1, 1) for e, c, s in zip(now, cots, mems)]
        zk = [-e * mm(x, s, 1, 1) for e, x, s in zip(now, xs, mems)]
        wg = [t * mm(w, g, 1, 1) for t, w, g in zip(tail, ws, grads)]
        dqn, dkn = None, None
        cross_sum, gram_sum = dcross[0], dgram[0]
        dqn, dkn = zq[0], bcol[0] * zk[0] + wg[0]
        for n in range(1, ratio):
            cross_sum, gram_sum = cross_sum + dcross[n], gram_sum + dgram[n]
            dqn, dkn = dqn + zq[n], dkn + bcol[n] * zk[n] + wg[n]
        dqn = dqn + mm(split(cross_sum), ks)
        dkn = dkn + mm(split(cross_sum.T), qs) + mm(split(gram_sum + gram_sum.T), ks)
        for raw, scale, dn, out in ((qn, qscale, dqn, dq_ref), (kn, kscale, dkn, dk_ref)):
            along = jnp.sum(raw * dn, axis=-1, keepdims=True)
            out[:, m * GDIM : (m + 1) * GDIM] = scale * (dn - raw * along)
        for n, v in enumerate(heads):
            dv_ref[:, v * GDIM : (v + 1) * GDIM] = bcol[n] * target[n]
            pairs = dcross[n] * cross + dgram[n] * gram
            kept = kn * wg[n]
            old = kn * zk[n]
            by_row = pairs + qn * zq[n] + bcol[n] * old - kept
            dgam_rows.append(jnp.sum(by_row.T - pairs, axis=0, keepdims=True))
            values = head_cols(v_ref, v).astype(F32)
            by_beta = dsys[n] * gram + target[n] * values + old
            dbeta_rows.append(jnp.sum(by_beta.T, axis=0, keepdims=True))
            both = kept + jnp.exp(lasts[n]) * (mem[n] * grad[n])
            ends.append(jnp.sum(jnp.sum(both, axis=0, keepdims=True), axis=1, keepdims=True))
    dlog = lane_cumsum(jnp.concatenate(dgam_rows, axis=0), True) + jnp.concatenate(ends, axis=0)
    dbeta = jnp.concatenate(dbeta_rows, axis=0)
    ddecay_ref[...] = -per_head(rate_ref, decay_ref) * sigmoid(decay_ref[...]) * dlog
    gate = sigmoid(write_ref[...])
    dwrite_ref[...] = per_head(scale_ref, write_ref) * gate * (1.0 - gate) * dbeta


def attention(lists_ref, q_ref, cot_ref, lse_ref, delta_ref, kv_ref, dq_ref, dkv_ref, q_all, cot_all):
    score_scale = HD ** (-0.5)
    me = lax.axis_index("ctx")
    tokens = q_ref.shape[0]
    heads = q_ref.shape[1] // HD
    blocks_here = tokens // BLK
    first = me * blocks_here
    for h in range(heads):
        q_all[h * tokens : (h + 1) * tokens, :] = q_ref[:, h * HD : (h + 1) * HD]
        cot_all[h * tokens : (h + 1) * tokens, :] = cot_ref[:, h * HD : (h + 1) * HD]
    dq_ref[...] = jnp.zeros_like(dq_ref)
    lane = lax.broadcasted_iota(jnp.int32, (1, tokens), 1)
    row_pos = me * tokens + lane
    row_block = row_pos // BLK
    mine = pl.ds(pl.multiple_of(me * tokens, tokens), tokens)

    def block(owner):
        q, cot = (q_all[...], None), (cot_all[...], None)
        k, v = (kv_ref[owner][:, :HD], None), (kv_ref[owner][:, HD:], None)
        key_pos = owner * tokens + lax.broadcasted_iota(jnp.int32, (tokens, tokens), 0)
        key_block = key_pos // BLK
        own = (key_block == row_block) & (key_pos <= row_pos)
        before = key_block < row_block
        scores = mm(k, q, 1, 1)
        dprobs = mm(v, cot, 1, 1)
        probs, dscores = [], []
        for h in range(heads):
            member = None
            for t in range(TOPK):
                entry = jnp.zeros((1, tokens), jnp.int32)
                for b in range(blocks_here):
                    listed = lists_ref[h, first + b, t]
                    entry = jnp.where(lane // BLK == b, listed, entry)
                hit = key_block == entry
                member = hit if member is None else member | hit
            allowed = own | (before & member)
            span = slice(h * tokens, (h + 1) * tokens)
            lse, delta = lse_ref[h : h + 1, mine], delta_ref[h : h + 1, mine]
            prob = jnp.where(allowed, jnp.exp(scores[:, span] * score_scale - lse), 0.0)
            probs.append(prob)
            dscores.append(prob * (dprobs[:, span] - delta) * score_scale)
        ds = split(jnp.concatenate(dscores, axis=1))
        dkv_ref[owner, :, :HD] = mm(ds, q)
        dkv_ref[owner, :, HD:] = mm(split(jnp.concatenate(probs, axis=1)), cot)
        dq = mm(ds, k, 0, 0)
        for h in range(heads):
            dq_ref[:, h * HD : (h + 1) * HD] += dq[h * tokens : (h + 1) * tokens]

    return block


def through_chain(
    lists_ref, aq_hbm, acot_hbm, lse_hbm, delta_hbm, ak_hbm, av_hbm,
    q_hbm, k_hbm, v_hbm, cot_hbm, decay_hbm, write_hbm, rate_ref, scale_ref,
    inv_ref, wu_ref, gam_ref, beta_ref, dq_ref, mem_ref, grad_ref, adk_ref, adv_ref,
    q_ref, k_ref, v_ref, cot_ref, decay_ref, write_ref,
    aq_ref, acot_ref, lse_ref, delta_ref, ak_ref, av_ref, load_sem,
    map_ref, mapt_ref, add_ref, pull_ref, kv, q_all, cot_all, dkv, twin_in, far_in, groups,
    mem_out, grad_out, far_send, far_recv, near_send, near_recv,
    mem_send, mem_recv, grad_send, grad_recv, pair_send, pair_recv, sum_send, sum_recv,
    group_send, group_recv,
):
    n = lax.axis_size("ctx")
    me, head_at = lax.axis_index("ctx"), lax.axis_index("head")
    heads = aq_ref.shape[1] // HD
    chips = n // 2
    loads = [
        pltpu.make_async_copy(source, target, load_sem.at[i])
        for i, (source, target) in enumerate(
            (
                (ak_hbm, ak_ref), (av_hbm, av_ref),
                (q_hbm, q_ref), (k_hbm, k_ref), (v_hbm, v_ref), (cot_hbm, cot_ref),
                (decay_hbm, decay_ref), (write_hbm, write_ref),
                (aq_hbm, aq_ref), (acot_hbm, acot_ref), (lse_hbm, lse_ref), (delta_hbm, delta_ref),
            )
        )
    ]
    for load in loads:
        load.start()
    twin = me + 1 - 2 * lax.rem(me, 2)
    barrier = pltpu.get_barrier_semaphore()
    for d in range(1, n):
        pl.semaphore_signal(
            barrier, inc=1, device_id=(lax.rem(me + d, n), head_at), device_id_type=MESH
        )
    others = lax.axis_size("head")
    for d in range(1, others):
        pl.semaphore_signal(
            barrier, inc=1, device_id=(me, lax.rem(head_at + d, others)), device_id_type=MESH
        )
    for load in loads[:2]:
        load.wait()
    pl.semaphore_wait(barrier, n + others - 2)

    group = head_at * heads // (Q_HEADS // KV_HEADS)
    columns = pl.ds(pl.multiple_of(group * HD, HD), HD)
    kv[me, :, :HD] = ak_ref[:, columns]
    kv[me, :, HD:] = av_ref[:, columns]

    def copy(slot, send_sem, recv_sem, index, to):
        return pltpu.make_async_remote_copy(
            src_ref=kv.at[slot],
            dst_ref=kv.at[slot],
            send_sem=send_sem.at[index],
            recv_sem=recv_sem.at[index],
            device_id=(to, head_at),
            device_id_type=MESH,
        )

    def source(d):
        return lax.rem(me + n - 2 * d, n)

    def far(d):
        return copy(me, far_send, far_recv, d, lax.rem(me + 2 * d, n))

    for d in range(1, chips):
        far(d).start()
    copy(me, near_send, near_recv, 0, twin).start()
    for load in loads[2:8]:
        load.wait()

    gdn_local(
        q_ref, k_ref, v_ref, cot_ref, decay_ref, write_ref, rate_ref, scale_ref,
        inv_ref, wu_ref, map_ref, mapt_ref, add_ref, pull_ref, gam_ref, beta_ref,
    )
    for load in loads[8:]:
        load.wait()
    block = attention(
        lists_ref, aq_ref, acot_ref, lse_ref, delta_ref, kv, dq_ref, dkv, q_all, cot_all
    )
    for d in range(1, chips):
        copy(source(d), far_send, far_recv, d, twin).wait_recv()
        copy(source(d), near_send, near_recv, d, twin).start()

    chip, core = lax.div(me, 2), lax.rem(me, 2)

    def pair(c):
        return pltpu.make_async_remote_copy(
            src_ref=dkv.at[2 * c + 1 - core],
            dst_ref=twin_in.at[c],
            send_sem=pair_send.at[c],
            recv_sem=pair_recv.at[c],
            device_id=(twin, head_at),
            device_id_type=MESH,
        )

    def down(c):
        return pltpu.make_async_remote_copy(
            src_ref=dkv.at[2 * c + core],
            dst_ref=far_in.at[chip - c],
            send_sem=sum_send.at[chip - c],
            recv_sem=sum_recv.at[chip - c],
            device_id=(2 * c + core, head_at),
            device_id_type=MESH,
        )

    def visit(start, to_twin):
        def turn(c, carry):
            owner = 2 * c + lax.rem(start, 2)

            @pl.when(owner <= me)
            def _():
                block(owner)
                if to_twin:
                    pair(c).start()

            return carry

        lax.fori_loop(0, chips, turn, 0)

    visit(me, False)
    for d in range(chips):
        copy(lax.rem(twin + n - 2 * d, n), near_send, near_recv, d, twin).wait_recv()
    visit(twin, True)

    def combine(c, carry):
        @pl.when(2 * c + core <= twin)
        def _():
            pair(c).wait_recv()
            dkv[2 * c + core] = dkv[2 * c + core] + twin_in[c]

        @pl.when(c < chip)
        def _():
            down(c).start()

        return carry

    lax.fori_loop(0, chips, combine, 0)

    def share(d):
        return pltpu.make_async_remote_copy(
            src_ref=groups.at[head_at],
            dst_ref=groups.at[head_at],
            send_sem=group_send.at[d],
            recv_sem=group_recv.at[d],
            device_id=(me, lax.rem(head_at + d, others)),
            device_id_type=MESH,
        )

    def finish_sum():
        groups[head_at] = dkv[me]

        def turn(d, carry):
            @pl.when(chip + d < chips)
            def _():
                pltpu.make_async_remote_copy(
                    src_ref=dkv.at[me],
                    dst_ref=far_in.at[d],
                    send_sem=sum_send.at[d],
                    recv_sem=sum_recv.at[d],
                    device_id=(twin, head_at),
                    device_id_type=MESH,
                ).wait_recv()
                groups[head_at] = groups[head_at] + far_in[d]

            return carry

        lax.fori_loop(1, chips, turn, 0)
        for d in range(1, others):
            share(d).start()

    right, left = lax.rem(me + 1, n), lax.rem(me + n - 1, n)
    value_heads = map_ref.shape[0]

    def send(source, target, send_sem, recv_sem, head, to):
        return pltpu.make_async_remote_copy(
            src_ref=source.at[head],
            dst_ref=target.at[head],
            send_sem=send_sem.at[head],
            recv_sem=recv_sem.at[head],
            device_id=(to, head_at),
            device_id_type=MESH,
        )

    def advance(head):
        copy = send(mem_out, mem_ref, mem_send, mem_recv, head, right)

        @pl.when(me == 0)
        def _():
            mem_ref[head] = jnp.zeros((GDIM, GDIM), F32)

        @pl.when(me > 0)
        def _():
            copy.wait_recv()

        @pl.when(me < n - 1)
        def _():
            mem_out[head] = mm(split(map_ref[head]), split(mem_ref[head])) + add_ref[head]
            copy.start()

    def retreat(head):
        copy = send(grad_out, grad_ref, grad_send, grad_recv, head, left)

        @pl.when(me == n - 1)
        def _():
            grad_ref[head] = jnp.zeros((GDIM, GDIM), F32)

        @pl.when(me < n - 1)
        def _():
            copy.wait_recv()

        @pl.when(me > 0)
        def _():
            grad_out[head] = mm(split(mapt_ref[head]), split(grad_ref[head])) + pull_ref[head]
            copy.start()

    steps = 2 * value_heads
    sum_at = jnp.minimum((chips - 1 - chip) * 5, steps - 1)
    lag = jnp.clip((n - 1 - 2 * me) * 3, -value_heads, value_heads)
    mem_late, grad_late = jnp.maximum(-lag, 0), jnp.maximum(lag, 0)

    def turn(step, carry):
        mem_head, grad_head = step - mem_late, step - grad_late

        @pl.when((mem_head >= 0) & (mem_head < value_heads))
        def _():
            advance(mem_head)

        @pl.when((grad_head >= 0) & (grad_head < value_heads))
        def _():
            retreat(grad_head)

        @pl.when(step == sum_at)
        def _():
            finish_sum()

        return carry

    lax.fori_loop(0, steps, turn, 0)

    def drain(head, carry):
        @pl.when(me < n - 1)
        def _():
            send(mem_out, mem_ref, mem_send, mem_recv, head, right).wait_send()

        @pl.when(me > 0)
        def _():
            send(grad_out, grad_ref, grad_send, grad_recv, head, left).wait_send()

        return carry

    lax.fori_loop(0, value_heads, drain, 0)

    def drain_sums(c, carry):
        @pl.when(2 * c + 1 - core <= me)
        def _():
            pair(c).wait_send()

        @pl.when(c < chip)
        def _():
            down(c).wait_send()

        return carry

    lax.fori_loop(0, chips, drain_sums, 0)
    for d in range(1, others):
        here = lax.rem(head_at + others - d, others)
        pltpu.make_async_remote_copy(
            src_ref=groups.at[here],
            dst_ref=groups.at[here],
            send_sem=group_send.at[d],
            recv_sem=group_recv.at[d],
            device_id=(me, here),
            device_id_type=MESH,
        ).wait_recv()
    each = others // KV_HEADS
    for c in range(KV_HEADS):
        total = groups[c * each]
        for d in range(1, each):
            total = total + groups[c * each + d]
        adk_ref[:, c * HD : (c + 1) * HD] = total[:, :HD]
        adv_ref[:, c * HD : (c + 1) * HD] = total[:, HD:]
    for d in range(1, others):
        share(d).wait_send()
    for d in range(1, chips):
        far(d).wait_send()
    for d in range(chips):
        copy(source(d), near_send, near_recv, d, twin).wait_send()


def on_device(
    attn_q, attn_k, attn_v, attn_cot, attn_lse, attn_delta, block_lists,
    gdn_q, gdn_k, gdn_v, decay_logit, write_logit, decay_rate, write_scale, gdn_cot,
):
    tokens = attn_q.shape[0]
    local_heads = attn_q.shape[1] // HD
    ctx = lax.axis_size("ctx")
    head_devices = lax.axis_size("head")
    value_heads = gdn_v.shape[1] // GDIM
    vmem, smem = (pl.BlockSpec(memory_space=space) for space in (pltpu.VMEM, pltpu.SMEM))

    square = jax.ShapeDtypeStruct((value_heads, GDIM, GDIM), F32)
    gates = jax.ShapeDtypeStruct((value_heads, tokens), F32)
    key_grads = jax.ShapeDtypeStruct((tokens, KV_HEADS * HD), F32)
    buffer = pltpu.VMEM((value_heads, GDIM, GDIM), F32)
    stacked = pltpu.VMEM((local_heads * tokens, HD), BF16)

    def sums(count, kind):
        return pltpu.VMEM((count, tokens, 2 * HD), kind)

    def sems(count):
        return pltpu.SemaphoreType.DMA((count,))

    attn_in = (attn_q, attn_cot, attn_lse, attn_delta, attn_k, attn_v)
    gdn_in = (gdn_q, gdn_k, gdn_v, gdn_cot, decay_logit, write_logit)
    chips = ctx // 2
    hbm = pl.BlockSpec(memory_space=pltpu.HBM)
    inverse, wu, gam, beta, grad_q, mem, grad, attn_dk, attn_dv = pl.pallas_call(
        through_chain,
        out_shape=(
            jax.ShapeDtypeStruct((value_heads, tokens, tokens), F32),
            jax.ShapeDtypeStruct((value_heads, tokens, 2 * GDIM), F32),
            gates, gates,
            jax.ShapeDtypeStruct((tokens, local_heads * HD), F32),
            square, square, key_grads, key_grads,
        ),
        in_specs=[smem] + [hbm] * 12 + [smem, smem],
        out_specs=[vmem] * 9,
        scratch_shapes=[pltpu.VMEM(x.shape, x.dtype) for x in gdn_in + attn_in]
        + [sems(12)]
        + [buffer] * 4
        + [sums(ctx, BF16), stacked, stacked, sums(ctx, F32), sums(chips, F32), sums(chips, F32)]
        + [sums(head_devices, F32), buffer, buffer]
        + [sems(chips)] * 4
        + [sems(value_heads)] * 4
        + [sems(chips)] * 4
        + [sems(head_devices)] * 2,
        compiler_params=pltpu.CompilerParams(
            collective_id=0, has_side_effects=True, vmem_limit_bytes=VMEM_BYTES
        ),
        name="through_chain",
    )(block_lists, *attn_in, *gdn_in, decay_rate, write_scale)

    dq, dk, dv, ddecay, dwrite = pl.pallas_call(
        gdn_grads,
        out_shape=(
            jax.ShapeDtypeStruct(gdn_q.shape, F32),
            jax.ShapeDtypeStruct(gdn_k.shape, F32),
            jax.ShapeDtypeStruct(gdn_v.shape, F32),
            gates, gates,
        ),
        in_specs=[vmem] * 6 + [smem, smem] + [vmem] * 6,
        out_specs=[vmem] * 5,
        compiler_params=pltpu.CompilerParams(vmem_limit_bytes=VMEM_BYTES),
        name="gdn_grads",
    )(*gdn_in, decay_rate, write_scale, inverse, wu, gam, beta, mem, grad)
    return (grad_q, attn_dk, attn_dv, dq, dk, dv, ddecay, dwrite)


def solution(mesh):
    return jax.shard_map(
        on_device,
        mesh=mesh,
        in_specs=(
            P("ctx", "head"), P("ctx", None), P("ctx", None), P("ctx", "head"),
            P("head", None), P("head", None), P("head", None, None),
            P("ctx", "head"), P("ctx", "head"), P("ctx", "head"),
            P("head", "ctx"), P("head", "ctx"), P("head"), P("head"), P("ctx", "head"),
        ),
        out_specs=(
            P("ctx", "head"), P("ctx", None), P("ctx", None),
            P("ctx", "head"), P("ctx", "head"), P("ctx", "head"),
            P("head", "ctx"), P("head", "ctx"),
        ),
        check_vma=False,
    )
```

```python
import jax
import jax.numpy as jnp
from jax import lax
from jax.experimental import pallas as pl
from jax.experimental.pallas import tpu as pltpu
from jax.sharding import PartitionSpec as P

Q_HEADS = 16
KV_HEADS = 2
HD = 256
GDIM = 128
BLK = 64
TOPK = 4
F32 = jnp.float32
BF16 = jnp.bfloat16
VMEM_BYTES = 58 * 1024 * 1024
MESH = pl.DeviceIdType.MESH


def split(x):
    if x.dtype == BF16:
        return (x, None)
    head = x.astype(BF16)
    return (head, (x - head.astype(F32)).astype(BF16))


def mm(a, b, ca=1, cb=0):
    dims = (((ca,), (cb,)), ((), ()))
    out = lax.dot_general(a[0], b[0], dims, preferred_element_type=F32)
    if b[1] is not None:
        out = out + lax.dot_general(a[0], b[1], dims, preferred_element_type=F32)
    if a[1] is not None:
        out = out + lax.dot_general(a[1], b[0], dims, preferred_element_type=F32)
    return out


def lane_cumsum(x, backward):
    width = x.shape[1]
    lanes = lax.broadcasted_iota(jnp.int32, x.shape, 1)
    step = 1
    while step < width:
        moved = pltpu.roll(x, width - step if backward else step, 1)
        keep = lanes < width - step if backward else lanes >= step
        x = x + jnp.where(keep, moved, 0.0)
        step *= 2
    return x


def softplus(x):
    return jnp.maximum(x, 0.0) + jnp.log(1.0 + jnp.exp(-jnp.abs(x)))


def sigmoid(x):
    return 1.0 / (1.0 + jnp.exp(-x))


def column_form(row, size):
    return jnp.broadcast_to(row, (size, size)).T


def unit_rows(raw):
    full = raw.astype(F32)
    scale = lax.rsqrt(jnp.sum(full * full, axis=-1, keepdims=True) + 1e-06)
    return full * scale, scale


def head_cols(ref, head):
    return ref[:, head * GDIM : (head + 1) * GDIM]


def per_head(ref, like):
    heads, width = like.shape
    return jnp.concatenate([jnp.full((1, width), ref[v], F32) for v in range(heads)], axis=0)


def triangles(size):
    rows = lax.broadcasted_iota(jnp.int32, (size, size), 0)
    cols = lax.broadcasted_iota(jnp.int32, (size, size), 1)
    return rows, cols


def gdn_local(
    q_ref, k_ref, v_ref, cot_ref, decay_ref, write_ref, rate_ref, scale_ref,
    inv_ref, wu_ref, map_ref, mapt_ref, add_ref, pull_ref, gam_ref, beta_ref,
):
    size = q_ref.shape[0]
    key_heads = q_ref.shape[1] // GDIM
    value_heads = v_ref.shape[1] // GDIM
    ratio = value_heads // key_heads
    gam = lane_cumsum(-per_head(rate_ref, decay_ref) * softplus(decay_ref[...]), False)
    beta = per_head(scale_ref, write_ref) * sigmoid(write_ref[...])
    gam_ref[...] = gam
    beta_ref[...] = beta
    rows, cols = triangles(size)
    eye = jnp.where(rows == cols, 1.0, 0.0)
    group = min(4, value_heads)
    for first in range(0, value_heads, group):
        heads = list(range(first, first + group))
        keyed = {}
        for m in sorted({v // ratio for v in heads}):
            qn, kn = unit_rows(head_cols(q_ref, m))[0], unit_rows(head_cols(k_ref, m))[0]
            qs, ks = split(qn), split(kn)
            keyed[m] = (qn, kn, mm(ks, ks, 1, 1), mm(qs, ks, 1, 1), split(kn.T))
        gcol = [column_form(gam[v : v + 1, :], size) for v in heads]
        bcol = [column_form(beta[v : v + 1, :], size) for v in heads]
        upto = [
            jnp.where(rows >= cols, jnp.exp(jnp.minimum(c - gam[v : v + 1, :], 0.0)), 0.0)
            for c, v in zip(gcol, heads)
        ]
        system = [
            jnp.where(rows > cols, b * u * keyed[v // ratio][2], 0.0)
            for b, u, v in zip(bcol, upto, heads)
        ]
        inverse = [eye - jnp.where(rows // 2 == cols // 2, s, 0.0) for s in system]
        half = 2
        while half < size:
            low = (rows // half == cols // half + 1) & ((rows // half) % 2 == 1)
            parts = [split(t) for t in inverse]
            inner = [mm(split(jnp.where(low, s, 0.0)), t) for s, t in zip(system, parts)]
            outer = [mm(t, split(x)) for t, x in zip(parts, inner)]
            inverse = [t - x for t, x in zip(inverse, outer)]
            half *= 2
        for n, v in enumerate(heads):
            qn, kn, gram, cross, knt = keyed[v // ratio]
            now = jnp.exp(gcol[n])
            inv_ref[v] = inverse[n]
            targets = jnp.concatenate(
                [bcol[n] * now * kn, bcol[n] * head_cols(v_ref, v).astype(F32)], axis=1
            )
            wu = mm(split(inverse[n]), split(targets))
            wu_ref[v] = wu
            last = gam[v : v + 1, size - 1 : size]
            tail = jnp.exp(last - gcol[n])
            ends = mm(knt, split(jnp.concatenate([tail, tail], axis=1) * wu))
            whole = jnp.exp(last) * eye - ends[:, :GDIM]
            map_ref[v] = whole
            mapt_ref[v] = whole.T
            add_ref[v] = ends[:, GDIM:]
            reads = now * qn - mm(split(upto[n] * cross), split(wu[:, :GDIM]))
            pull_ref[v] = mm(split(reads.T), split(head_cols(cot_ref, v)))


def gdn_grads(
    q_ref, k_ref, v_ref, cot_ref, decay_ref, write_ref, rate_ref, scale_ref,
    inv_ref, wu_ref, gam_ref, beta_ref, mem_ref, grad_ref,
    dq_ref, dk_ref, dv_ref, ddecay_ref, dwrite_ref, after_head,
):
    size = q_ref.shape[0]
    key_heads = q_ref.shape[1] // GDIM
    value_heads = v_ref.shape[1] // GDIM
    ratio = value_heads // key_heads
    rows, cols = triangles(size)
    gam, beta = gam_ref[...], beta_ref[...]
    dgam_rows, dbeta_rows, ends = [], [], []
    for m in range(key_heads):
        heads = list(range(m * ratio, (m + 1) * ratio))
        qn, qscale = unit_rows(head_cols(q_ref, m))
        kn, kscale = unit_rows(head_cols(k_ref, m))
        qs, ks = split(qn), split(kn)
        gram, cross = mm(ks, ks, 1, 1), mm(qs, ks, 1, 1)
        gcol = [column_form(gam[v : v + 1, :], size) for v in heads]
        bcol = [column_form(beta[v : v + 1, :], size) for v in heads]
        lasts = [gam[v : v + 1, size - 1 : size] for v in heads]
        now = [jnp.exp(c) for c in gcol]
        tail = [jnp.exp(e - c) for e, c in zip(lasts, gcol)]
        upto = [
            jnp.where(rows >= cols, jnp.exp(jnp.minimum(c - gam[v : v + 1, :], 0.0)), 0.0)
            for c, v in zip(gcol, heads)
        ]
        strict = [jnp.where(rows > cols, u, 0.0) for u in upto]
        mem = [mem_ref[v] for v in heads]
        grad = [grad_ref[v] for v in heads]
        mems, grads = [split(x) for x in mem], [split(x) for x in grad]
        cots = [split(head_cols(cot_ref, v)) for v in heads]
        written = [
            wu_ref[v][:, GDIM:] - mm(split(wu_ref[v][:, :GDIM]), s) for v, s in zip(heads, mems)
        ]
        ws = [split(w) for w in written]
        dwritten = [
            mm(split((u * cross).T), c) + t * mm(ks, g)
            for u, c, t, g in zip(upto, cots, tail, grads)
        ]
        target = [mm(split(inv_ref[v].T), split(d)) for v, d in zip(heads, dwritten)]
        xs = [split(x) for x in target]
        dcross = [u * mm(c, w, 1, 1) for u, c, w in zip(upto, cots, ws)]
        dsys = [-s * mm(x, w, 1, 1) for s, x, w in zip(strict, xs, ws)]
        dgram = [b * d for b, d in zip(bcol, dsys)]
        zq = [e * mm(c, s, 1, 1) for e, c, s in zip(now, cots, mems)]
        zk = [-e * mm(x, s, 1, 1) for e, x, s in zip(now, xs, mems)]
        wg = [t * mm(w, g, 1, 1) for t, w, g in zip(tail, ws, grads)]
        dqn, dkn = None, None
        cross_sum, gram_sum = dcross[0], dgram[0]
        dqn, dkn = zq[0], bcol[0] * zk[0] + wg[0]
        for n in range(1, ratio):
            cross_sum, gram_sum = cross_sum + dcross[n], gram_sum + dgram[n]
            dqn, dkn = dqn + zq[n], dkn + bcol[n] * zk[n] + wg[n]
        dqn = dqn + mm(split(cross_sum), ks)
        dkn = dkn + mm(split(cross_sum.T), qs) + mm(split(gram_sum + gram_sum.T), ks)
        for raw, scale, dn, out in ((qn, qscale, dqn, dq_ref), (kn, kscale, dkn, dk_ref)):
            along = jnp.sum(raw * dn, axis=-1, keepdims=True)
            out[:, m * GDIM : (m + 1) * GDIM] = scale * (dn - raw * along)
        for n, v in enumerate(heads):
            dv_ref[:, v * GDIM : (v + 1) * GDIM] = bcol[n] * target[n]
            pairs = dcross[n] * cross + dgram[n] * gram
            kept = kn * wg[n]
            old = kn * zk[n]
            by_row = pairs + qn * zq[n] + bcol[n] * old - kept
            dgam_rows.append(jnp.sum(by_row.T - pairs, axis=0, keepdims=True))
            values = head_cols(v_ref, v).astype(F32)
            by_beta = dsys[n] * gram + target[n] * values + old
            dbeta_rows.append(jnp.sum(by_beta.T, axis=0, keepdims=True))
            both = kept + jnp.exp(lasts[n]) * (mem[n] * grad[n])
            ends.append(jnp.sum(jnp.sum(both, axis=0, keepdims=True), axis=1, keepdims=True))
        after_head(m)
    dlog = lane_cumsum(jnp.concatenate(dgam_rows, axis=0), True) + jnp.concatenate(ends, axis=0)
    dbeta = jnp.concatenate(dbeta_rows, axis=0)
    ddecay_ref[...] = -per_head(rate_ref, decay_ref) * sigmoid(decay_ref[...]) * dlog
    gate = sigmoid(write_ref[...])
    dwrite_ref[...] = per_head(scale_ref, write_ref) * gate * (1.0 - gate) * dbeta


def attention(lists_ref, q_ref, cot_ref, lse_ref, delta_ref, kv_ref, dq_ref, dkv_ref, q_all, cot_all):
    score_scale = HD ** (-0.5)
    me = lax.axis_index("ctx")
    tokens = q_ref.shape[0]
    heads = q_ref.shape[1] // HD
    blocks_here = tokens // BLK
    first = me * blocks_here
    for h in range(heads):
        q_all[h * tokens : (h + 1) * tokens, :] = q_ref[:, h * HD : (h + 1) * HD]
        cot_all[h * tokens : (h + 1) * tokens, :] = cot_ref[:, h * HD : (h + 1) * HD]
    dq_ref[...] = jnp.zeros_like(dq_ref)
    lane = lax.broadcasted_iota(jnp.int32, (1, tokens), 1)
    row_pos = me * tokens + lane
    row_block = row_pos // BLK
    mine = pl.ds(pl.multiple_of(me * tokens, tokens), tokens)

    def block(owner):
        q, cot = (q_all[...], None), (cot_all[...], None)
        k, v = (kv_ref[owner][:, :HD], None), (kv_ref[owner][:, HD:], None)
        key_pos = owner * tokens + lax.broadcasted_iota(jnp.int32, (tokens, tokens), 0)
        key_block = key_pos // BLK
        own = (key_block == row_block) & (key_pos <= row_pos)
        before = key_block < row_block
        scores = mm(k, q, 1, 1)
        dprobs = mm(v, cot, 1, 1)
        probs, dscores = [], []
        for h in range(heads):
            member = None
            for t in range(TOPK):
                entry = jnp.zeros((1, tokens), jnp.int32)
                for b in range(blocks_here):
                    listed = lists_ref[h, t, first + b]
                    entry = jnp.where(lane // BLK == b, listed, entry)
                hit = key_block == entry
                member = hit if member is None else member | hit
            allowed = own | (before & member)
            span = slice(h * tokens, (h + 1) * tokens)
            lse, delta = lse_ref[h : h + 1, mine], delta_ref[h : h + 1, mine]
            prob = jnp.where(allowed, jnp.exp(scores[:, span] * score_scale - lse), 0.0)
            probs.append(prob)
            dscores.append(prob * (dprobs[:, span] - delta) * score_scale)
        ds = split(jnp.concatenate(dscores, axis=1))
        dkv_ref[owner, :, :HD] = mm(ds, q)
        dkv_ref[owner, :, HD:] = mm(split(jnp.concatenate(probs, axis=1)), cot)
        dq = mm(ds, k, 0, 0)
        for h in range(heads):
            dq_ref[:, h * HD : (h + 1) * HD] += dq[h * tokens : (h + 1) * tokens]

    return block


def through_chain(
    lists_ref, aq_hbm, acot_hbm, lse_hbm, delta_hbm, ak_hbm, av_hbm,
    q_hbm, k_hbm, v_hbm, cot_hbm, decay_hbm, write_hbm, rate_ref, scale_ref,
    dq_ref, adk_ref, adv_ref, gdq_ref, gdk_ref, gdv_ref, ddecay_ref, dwrite_ref,
    inv_ref, wu_ref, gam_ref, beta_ref, mem_ref, grad_ref,
    q_ref, k_ref, v_ref, cot_ref, decay_ref, write_ref,
    aq_ref, acot_ref, lse_ref, delta_ref, ak_ref, av_ref, load_sem,
    map_ref, mapt_ref, add_ref, pull_ref, kv, q_all, cot_all, dkv, twin_in, far_in, groups,
    mem_out, grad_out, far_send, far_recv, near_send, near_recv,
    mem_send, mem_recv, grad_send, grad_recv, pair_send, pair_recv, sum_send, sum_recv,
    group_send, group_recv,
):
    n = lax.axis_size("ctx")
    me, head_at = lax.axis_index("ctx"), lax.axis_index("head")
    heads = aq_ref.shape[1] // HD
    chips = n // 2
    loads = [
        pltpu.make_async_copy(source, target, load_sem.at[i])
        for i, (source, target) in enumerate(
            (
                (ak_hbm, ak_ref), (av_hbm, av_ref),
                (q_hbm, q_ref), (k_hbm, k_ref), (v_hbm, v_ref), (cot_hbm, cot_ref),
                (decay_hbm, decay_ref), (write_hbm, write_ref),
                (aq_hbm, aq_ref), (acot_hbm, acot_ref), (lse_hbm, lse_ref), (delta_hbm, delta_ref),
            )
        )
    ]
    for load in loads:
        load.start()
    twin = me + 1 - 2 * lax.rem(me, 2)
    barrier = pltpu.get_barrier_semaphore()
    for d in range(1, n):
        pl.semaphore_signal(
            barrier, inc=1, device_id=(lax.rem(me + d, n), head_at), device_id_type=MESH
        )
    others = lax.axis_size("head")
    for d in range(1, others):
        pl.semaphore_signal(
            barrier, inc=1, device_id=(me, lax.rem(head_at + d, others)), device_id_type=MESH
        )
    for load in loads[:2]:
        load.wait()
    pl.semaphore_wait(barrier, n + others - 2)

    group = head_at * heads // (Q_HEADS // KV_HEADS)
    columns = pl.ds(pl.multiple_of(group * HD, HD), HD)
    kv[me, :, :HD] = ak_ref[:, columns]
    kv[me, :, HD:] = av_ref[:, columns]

    def copy(slot, send_sem, recv_sem, index, to):
        return pltpu.make_async_remote_copy(
            src_ref=kv.at[slot],
            dst_ref=kv.at[slot],
            send_sem=send_sem.at[index],
            recv_sem=recv_sem.at[index],
            device_id=(to, head_at),
            device_id_type=MESH,
        )

    def source(d):
        return lax.rem(me + n - 2 * d, n)

    def far(d):
        return copy(me, far_send, far_recv, d, lax.rem(me + 2 * d, n))

    for d in range(1, chips):
        far(d).start()
    copy(me, near_send, near_recv, 0, twin).start()
    for load in loads[2:8]:
        load.wait()

    gdn_local(
        q_ref, k_ref, v_ref, cot_ref, decay_ref, write_ref, rate_ref, scale_ref,
        inv_ref, wu_ref, map_ref, mapt_ref, add_ref, pull_ref, gam_ref, beta_ref,
    )
    for load in loads[8:]:
        load.wait()
    block = attention(
        lists_ref, aq_ref, acot_ref, lse_ref, delta_ref, kv, dq_ref, dkv, q_all, cot_all
    )
    for d in range(1, chips):
        copy(source(d), far_send, far_recv, d, twin).wait_recv()
        copy(source(d), near_send, near_recv, d, twin).start()

    chip, core = lax.div(me, 2), lax.rem(me, 2)

    def pair(c):
        return pltpu.make_async_remote_copy(
            src_ref=dkv.at[2 * c + 1 - core],
            dst_ref=twin_in.at[c],
            send_sem=pair_send.at[c],
            recv_sem=pair_recv.at[c],
            device_id=(twin, head_at),
            device_id_type=MESH,
        )

    def down(c):
        return pltpu.make_async_remote_copy(
            src_ref=dkv.at[2 * c + core],
            dst_ref=far_in.at[chip - c],
            send_sem=sum_send.at[chip - c],
            recv_sem=sum_recv.at[chip - c],
            device_id=(2 * c + core, head_at),
            device_id_type=MESH,
        )

    def visit(start, to_twin):
        def turn(c, carry):
            owner = 2 * c + lax.rem(start, 2)

            @pl.when(owner <= me)
            def _():
                block(owner)
                if to_twin:
                    pair(c).start()

            return carry

        lax.fori_loop(0, chips, turn, 0)

    visit(me, False)
    for d in range(chips):
        copy(lax.rem(twin + n - 2 * d, n), near_send, near_recv, d, twin).wait_recv()
    visit(twin, True)

    def combine(c, carry):
        @pl.when(2 * c + core <= twin)
        def _():
            pair(c).wait_recv()
            dkv[2 * c + core] = dkv[2 * c + core] + twin_in[c]

        return carry

    lax.fori_loop(0, chips, combine, 0)

    def send_down():
        def turn(c, carry):
            @pl.when(c < chip)
            def _():
                down(c).start()

            return carry

        lax.fori_loop(0, chips, turn, 0)

    early = 2 * chip < chips

    @pl.when(early)
    def _():
        send_down()

    def share(d):
        return pltpu.make_async_remote_copy(
            src_ref=groups.at[head_at],
            dst_ref=groups.at[head_at],
            send_sem=group_send.at[d],
            recv_sem=group_recv.at[d],
            device_id=(me, lax.rem(head_at + d, others)),
            device_id_type=MESH,
        )

    def finish_sum():
        groups[head_at] = dkv[me]

        def turn(d, carry):
            @pl.when(chip + d < chips)
            def _():
                pltpu.make_async_remote_copy(
                    src_ref=dkv.at[me],
                    dst_ref=far_in.at[d],
                    send_sem=sum_send.at[d],
                    recv_sem=sum_recv.at[d],
                    device_id=(twin, head_at),
                    device_id_type=MESH,
                ).wait_recv()
                groups[head_at] = groups[head_at] + far_in[d]

            return carry

        lax.fori_loop(1, chips, turn, 0)
        for d in range(1, others):
            share(d).start()

    right, left = lax.rem(me + 1, n), lax.rem(me + n - 1, n)
    value_heads = map_ref.shape[0]

    def send(source, target, send_sem, recv_sem, head, to):
        return pltpu.make_async_remote_copy(
            src_ref=source.at[head],
            dst_ref=target.at[head],
            send_sem=send_sem.at[head],
            recv_sem=recv_sem.at[head],
            device_id=(to, head_at),
            device_id_type=MESH,
        )

    def advance(head):
        copy = send(mem_out, mem_ref, mem_send, mem_recv, head, right)

        @pl.when(me == 0)
        def _():
            mem_ref[head] = jnp.zeros((GDIM, GDIM), F32)

        @pl.when(me > 0)
        def _():
            copy.wait_recv()

        @pl.when(me < n - 1)
        def _():
            mem_out[head] = mm(split(map_ref[head]), split(mem_ref[head])) + add_ref[head]
            copy.start()

    def retreat(head):
        copy = send(grad_out, grad_ref, grad_send, grad_recv, head, left)

        @pl.when(me == n - 1)
        def _():
            grad_ref[head] = jnp.zeros((GDIM, GDIM), F32)

        @pl.when(me < n - 1)
        def _():
            copy.wait_recv()

        @pl.when(me > 0)
        def _():
            grad_out[head] = mm(split(mapt_ref[head]), split(grad_ref[head])) + pull_ref[head]
            copy.start()

    steps = 2 * value_heads
    lag = jnp.clip((n - 1 - 2 * me) * 3, -value_heads, value_heads)
    mem_late, grad_late = jnp.maximum(-lag, 0), jnp.maximum(lag, 0)

    def turn(step, carry):
        mem_head, grad_head = step - mem_late, step - grad_late

        @pl.when((mem_head >= 0) & (mem_head < value_heads))
        def _():
            advance(mem_head)

        @pl.when((grad_head >= 0) & (grad_head < value_heads))
        def _():
            retreat(grad_head)

        @pl.when((step == value_heads - 1) & jnp.logical_not(early))
        def _():
            send_down()

        return carry

    lax.fori_loop(0, steps, turn, 0)

    def after_head(m):
        @pl.when(sum_slot == m + 1)
        def _():
            finish_sum()

    sum_slot = jnp.minimum(chips - 1 - chip, q_ref.shape[1] // GDIM)
    after_head(-1)
    gdn_grads(
        q_ref, k_ref, v_ref, cot_ref, decay_ref, write_ref, rate_ref, scale_ref,
        inv_ref, wu_ref, gam_ref, beta_ref, mem_ref, grad_ref,
        gdq_ref, gdk_ref, gdv_ref, ddecay_ref, dwrite_ref, after_head,
    )

    def drain(head, carry):
        @pl.when(me < n - 1)
        def _():
            send(mem_out, mem_ref, mem_send, mem_recv, head, right).wait_send()

        @pl.when(me > 0)
        def _():
            send(grad_out, grad_ref, grad_send, grad_recv, head, left).wait_send()

        return carry

    lax.fori_loop(0, value_heads, drain, 0)

    def drain_sums(c, carry):
        @pl.when(2 * c + 1 - core <= me)
        def _():
            pair(c).wait_send()

        @pl.when(c < chip)
        def _():
            down(c).wait_send()

        return carry

    lax.fori_loop(0, chips, drain_sums, 0)
    for d in range(1, others):
        here = lax.rem(head_at + others - d, others)
        pltpu.make_async_remote_copy(
            src_ref=groups.at[here],
            dst_ref=groups.at[here],
            send_sem=group_send.at[d],
            recv_sem=group_recv.at[d],
            device_id=(me, here),
            device_id_type=MESH,
        ).wait_recv()
    each = others // KV_HEADS
    for c in range(KV_HEADS):
        total = groups[c * each]
        for d in range(1, each):
            total = total + groups[c * each + d]
        adk_ref[:, c * HD : (c + 1) * HD] = total[:, :HD]
        adv_ref[:, c * HD : (c + 1) * HD] = total[:, HD:]
    for d in range(1, others):
        share(d).wait_send()
    for d in range(1, chips):
        far(d).wait_send()
    for d in range(chips):
        copy(source(d), near_send, near_recv, d, twin).wait_send()


def hand_over(*refs):
    count = len(refs) // 2
    copies = [
        pltpu.make_async_copy(refs[i], refs[count + i], refs[-1].at[i]) for i in range(count)
    ]
    for copy in copies:
        copy.start()
    for copy in copies:
        copy.wait()


def on_device(
    attn_q, attn_k, attn_v, attn_cot, attn_lse, attn_delta, block_lists,
    gdn_q, gdn_k, gdn_v, decay_logit, write_logit, decay_rate, write_scale, gdn_cot,
):
    tokens = attn_q.shape[0]
    local_heads = attn_q.shape[1] // HD
    ctx = lax.axis_size("ctx")
    head_devices = lax.axis_size("head")
    value_heads = gdn_v.shape[1] // GDIM
    vmem, smem = (pl.BlockSpec(memory_space=space) for space in (pltpu.VMEM, pltpu.SMEM))

    gates = jax.ShapeDtypeStruct((value_heads, tokens), F32)
    key_grads = jax.ShapeDtypeStruct((tokens, KV_HEADS * HD), F32)
    buffer = pltpu.VMEM((value_heads, GDIM, GDIM), F32)
    stacked = pltpu.VMEM((local_heads * tokens, HD), BF16)

    def sums(count, kind):
        return pltpu.VMEM((count, tokens, 2 * HD), kind)

    def sems(count):
        return pltpu.SemaphoreType.DMA((count,))

    attn_in = (attn_q, attn_cot, attn_lse, attn_delta, attn_k, attn_v)
    gdn_in = (gdn_q, gdn_k, gdn_v, gdn_cot, decay_logit, write_logit)
    chips = ctx // 2
    hbm = pl.BlockSpec(memory_space=pltpu.HBM)
    results = (
        jax.ShapeDtypeStruct(attn_q.shape, F32),
        key_grads, key_grads,
        *(jax.ShapeDtypeStruct(x.shape, F32) for x in (gdn_q, gdn_k, gdn_v)),
        gates, gates,
    )
    held = pl.pallas_call(
        through_chain,
        out_shape=results,
        in_specs=[smem] + [hbm] * 12 + [smem, smem],
        out_specs=[vmem] * 8,
        scratch_shapes=[
            pltpu.VMEM((value_heads, tokens, tokens), F32),
            pltpu.VMEM((value_heads, tokens, 2 * GDIM), F32),
            pltpu.VMEM(gates.shape, F32),
            pltpu.VMEM(gates.shape, F32),
            buffer, buffer,
        ]
        + [pltpu.VMEM(x.shape, x.dtype) for x in gdn_in + attn_in]
        + [sems(12)]
        + [buffer] * 4
        + [sums(ctx, BF16), stacked, stacked, sums(ctx, F32), sums(chips, F32), sums(chips, F32)]
        + [sums(head_devices, F32), buffer, buffer]
        + [sems(chips)] * 4
        + [sems(value_heads)] * 4
        + [sems(chips)] * 4
        + [sems(head_devices)] * 2,
        compiler_params=pltpu.CompilerParams(
            collective_id=0, has_side_effects=True, vmem_limit_bytes=VMEM_BYTES
        ),
        name="through_chain",
    )(block_lists.transpose(0, 2, 1), *attn_in, *gdn_in, decay_rate, write_scale)

    return pl.pallas_call(
        hand_over,
        out_shape=results,
        in_specs=[hbm] * len(results),
        out_specs=[hbm] * len(results),
        scratch_shapes=[sems(len(results))],
        compiler_params=pltpu.CompilerParams(vmem_limit_bytes=VMEM_BYTES),
        name="hand_over",
    )(*held)


def solution(mesh):
    return jax.shard_map(
        on_device,
        mesh=mesh,
        in_specs=(
            P("ctx", "head"), P("ctx", None), P("ctx", None), P("ctx", "head"),
            P("head", None), P("head", None), P("head", None, None),
            P("ctx", "head"), P("ctx", "head"), P("ctx", "head"),
            P("head", "ctx"), P("head", "ctx"), P("head"), P("head"), P("ctx", "head"),
        ),
        out_specs=(
            P("ctx", "head"), P("ctx", None), P("ctx", None),
            P("ctx", "head"), P("ctx", "head"), P("ctx", "head"),
            P("head", "ctx"), P("head", "ctx"),
        ),
        check_vma=False,
    )
```

```python
import jax
import jax.numpy as jnp
from jax import lax
from jax.experimental import pallas as pl
from jax.experimental.pallas import tpu as pltpu
from jax.sharding import PartitionSpec as P

Q_HEADS = 16
KV_HEADS = 2
HD = 256
GDIM = 128
BLK = 64
TOPK = 4
F32 = jnp.float32
BF16 = jnp.bfloat16
VMEM_BYTES = 58 * 1024 * 1024
MESH = pl.DeviceIdType.MESH


def split(x):
    if x.dtype == BF16:
        return (x, None)
    head = x.astype(BF16)
    return (head, (x - head.astype(F32)).astype(BF16))


def mm(a, b, ca=1, cb=0):
    dims = (((ca,), (cb,)), ((), ()))
    out = lax.dot_general(a[0], b[0], dims, preferred_element_type=F32)
    if b[1] is not None:
        out = out + lax.dot_general(a[0], b[1], dims, preferred_element_type=F32)
    if a[1] is not None:
        out = out + lax.dot_general(a[1], b[0], dims, preferred_element_type=F32)
    return out


def lane_cumsum(x, backward):
    width = x.shape[1]
    lanes = lax.broadcasted_iota(jnp.int32, x.shape, 1)
    step = 1
    while step < width:
        moved = pltpu.roll(x, width - step if backward else step, 1)
        keep = lanes < width - step if backward else lanes >= step
        x = x + jnp.where(keep, moved, 0.0)
        step *= 2
    return x


def softplus(x):
    return jnp.maximum(x, 0.0) + jnp.log(1.0 + jnp.exp(-jnp.abs(x)))


def sigmoid(x):
    return 1.0 / (1.0 + jnp.exp(-x))


def column_form(row, size):
    return jnp.broadcast_to(row, (size, size)).T


def unit_rows(raw):
    full = raw.astype(F32)
    scale = lax.rsqrt(jnp.sum(full * full, axis=-1, keepdims=True) + 1e-06)
    return full * scale, scale


def head_cols(ref, head):
    return ref[:, head * GDIM : (head + 1) * GDIM]


def per_head(ref, like):
    heads, width = like.shape
    return jnp.concatenate([jnp.full((1, width), ref[v], F32) for v in range(heads)], axis=0)


def triangles(size):
    rows = lax.broadcasted_iota(jnp.int32, (size, size), 0)
    cols = lax.broadcasted_iota(jnp.int32, (size, size), 1)
    return rows, cols


def gdn_local(
    q_ref, k_ref, v_ref, cot_ref, decay_ref, write_ref, rate_ref, scale_ref,
    inv_ref, wu_ref, map_ref, mapt_ref, add_ref, pull_ref, gam_ref, beta_ref,
):
    size = q_ref.shape[0]
    key_heads = q_ref.shape[1] // GDIM
    value_heads = v_ref.shape[1] // GDIM
    ratio = value_heads // key_heads
    gam = lane_cumsum(-per_head(rate_ref, decay_ref) * softplus(decay_ref[...]), False)
    beta = per_head(scale_ref, write_ref) * sigmoid(write_ref[...])
    gam_ref[...] = gam
    beta_ref[...] = beta
    rows, cols = triangles(size)
    eye = jnp.where(rows == cols, 1.0, 0.0)
    group = min(4, value_heads)
    for first in range(0, value_heads, group):
        heads = list(range(first, first + group))
        keyed = {}
        for m in sorted({v // ratio for v in heads}):
            qn, kn = unit_rows(head_cols(q_ref, m))[0], unit_rows(head_cols(k_ref, m))[0]
            qs, ks = split(qn), split(kn)
            keyed[m] = (qn, kn, mm(ks, ks, 1, 1), mm(qs, ks, 1, 1), split(kn.T))
        gcol = [column_form(gam[v : v + 1, :], size) for v in heads]
        bcol = [column_form(beta[v : v + 1, :], size) for v in heads]
        upto = [
            jnp.where(rows >= cols, jnp.exp(jnp.minimum(c - gam[v : v + 1, :], 0.0)), 0.0)
            for c, v in zip(gcol, heads)
        ]
        system = [
            jnp.where(rows > cols, b * u * keyed[v // ratio][2], 0.0)
            for b, u, v in zip(bcol, upto, heads)
        ]
        inverse = [eye - jnp.where(rows // 2 == cols // 2, s, 0.0) for s in system]
        half = 2
        while half < size:
            low = (rows // half == cols // half + 1) & ((rows // half) % 2 == 1)
            parts = [split(t) for t in inverse]
            inner = [mm(split(jnp.where(low, s, 0.0)), t) for s, t in zip(system, parts)]
            outer = [mm(t, split(x)) for t, x in zip(parts, inner)]
            inverse = [t - x for t, x in zip(inverse, outer)]
            half *= 2
        for n, v in enumerate(heads):
            qn, kn, gram, cross, knt = keyed[v // ratio]
            now = jnp.exp(gcol[n])
            inv_ref[v] = inverse[n]
            targets = jnp.concatenate(
                [bcol[n] * now * kn, bcol[n] * head_cols(v_ref, v).astype(F32)], axis=1
            )
            wu = mm(split(inverse[n]), split(targets))
            wu_ref[v] = wu
            last = gam[v : v + 1, size - 1 : size]
            tail = jnp.exp(last - gcol[n])
            ends = mm(knt, split(jnp.concatenate([tail, tail], axis=1) * wu))
            whole = jnp.exp(last) * eye - ends[:, :GDIM]
            map_ref[v] = whole
            mapt_ref[v] = whole.T
            add_ref[v] = ends[:, GDIM:]
            reads = now * qn - mm(split(upto[n] * cross), split(wu[:, :GDIM]))
            pull_ref[v] = mm(split(reads.T), split(head_cols(cot_ref, v)))


def gdn_grads(
    q_ref, k_ref, v_ref, cot_ref, decay_ref, write_ref, rate_ref, scale_ref,
    inv_ref, wu_ref, gam_ref, beta_ref, mem_ref, grad_ref,
    dq_ref, dk_ref, dv_ref, ddecay_ref, dwrite_ref, after_head,
):
    size = q_ref.shape[0]
    key_heads = q_ref.shape[1] // GDIM
    value_heads = v_ref.shape[1] // GDIM
    ratio = value_heads // key_heads
    rows, cols = triangles(size)
    gam, beta = gam_ref[...], beta_ref[...]
    dgam_rows, dbeta_rows, ends = [], [], []
    for m in range(key_heads):
        heads = list(range(m * ratio, (m + 1) * ratio))
        qn, qscale = unit_rows(head_cols(q_ref, m))
        kn, kscale = unit_rows(head_cols(k_ref, m))
        qs, ks = split(qn), split(kn)
        gram, cross = mm(ks, ks, 1, 1), mm(qs, ks, 1, 1)
        gcol = [column_form(gam[v : v + 1, :], size) for v in heads]
        bcol = [column_form(beta[v : v + 1, :], size) for v in heads]
        lasts = [gam[v : v + 1, size - 1 : size] for v in heads]
        now = [jnp.exp(c) for c in gcol]
        tail = [jnp.exp(e - c) for e, c in zip(lasts, gcol)]
        upto = [
            jnp.where(rows >= cols, jnp.exp(jnp.minimum(c - gam[v : v + 1, :], 0.0)), 0.0)
            for c, v in zip(gcol, heads)
        ]
        strict = [jnp.where(rows > cols, u, 0.0) for u in upto]
        mem = [mem_ref[v] for v in heads]
        grad = [grad_ref[v] for v in heads]
        mems, grads = [split(x) for x in mem], [split(x) for x in grad]
        cots = [split(head_cols(cot_ref, v)) for v in heads]
        written = [
            wu_ref[v][:, GDIM:] - mm(split(wu_ref[v][:, :GDIM]), s) for v, s in zip(heads, mems)
        ]
        ws = [split(w) for w in written]
        dwritten = [
            mm(split((u * cross).T), c) + t * mm(ks, g)
            for u, c, t, g in zip(upto, cots, tail, grads)
        ]
        target = [mm(split(inv_ref[v].T), split(d)) for v, d in zip(heads, dwritten)]
        xs = [split(x) for x in target]
        dcross = [u * mm(c, w, 1, 1) for u, c, w in zip(upto, cots, ws)]
        dsys = [-s * mm(x, w, 1, 1) for s, x, w in zip(strict, xs, ws)]
        dgram = [b * d for b, d in zip(bcol, dsys)]
        zq = [e * mm(c, s, 1, 1) for e, c, s in zip(now, cots, mems)]
        zk = [-e * mm(x, s, 1, 1) for e, x, s in zip(now, xs, mems)]
        wg = [t * mm(w, g, 1, 1) for t, w, g in zip(tail, ws, grads)]
        dqn, dkn = None, None
        cross_sum, gram_sum = dcross[0], dgram[0]
        dqn, dkn = zq[0], bcol[0] * zk[0] + wg[0]
        for n in range(1, ratio):
            cross_sum, gram_sum = cross_sum + dcross[n], gram_sum + dgram[n]
            dqn, dkn = dqn + zq[n], dkn + bcol[n] * zk[n] + wg[n]
        dqn = dqn + mm(split(cross_sum), ks)
        dkn = dkn + mm(split(cross_sum.T), qs) + mm(split(gram_sum + gram_sum.T), ks)
        for raw, scale, dn, out in ((qn, qscale, dqn, dq_ref), (kn, kscale, dkn, dk_ref)):
            along = jnp.sum(raw * dn, axis=-1, keepdims=True)
            out[:, m * GDIM : (m + 1) * GDIM] = scale * (dn - raw * along)
        for n, v in enumerate(heads):
            dv_ref[:, v * GDIM : (v + 1) * GDIM] = bcol[n] * target[n]
            pairs = dcross[n] * cross + dgram[n] * gram
            kept = kn * wg[n]
            old = kn * zk[n]
            by_row = pairs + qn * zq[n] + bcol[n] * old - kept
            dgam_rows.append(jnp.sum(by_row.T - pairs, axis=0, keepdims=True))
            values = head_cols(v_ref, v).astype(F32)
            by_beta = dsys[n] * gram + target[n] * values + old
            dbeta_rows.append(jnp.sum(by_beta.T, axis=0, keepdims=True))
            both = kept + jnp.exp(lasts[n]) * (mem[n] * grad[n])
            ends.append(jnp.sum(jnp.sum(both, axis=0, keepdims=True), axis=1, keepdims=True))
        after_head(m)
    dlog = lane_cumsum(jnp.concatenate(dgam_rows, axis=0), True) + jnp.concatenate(ends, axis=0)
    dbeta = jnp.concatenate(dbeta_rows, axis=0)
    ddecay_ref[...] = -per_head(rate_ref, decay_ref) * sigmoid(decay_ref[...]) * dlog
    gate = sigmoid(write_ref[...])
    dwrite_ref[...] = per_head(scale_ref, write_ref) * gate * (1.0 - gate) * dbeta


def attention(lists_ref, q_ref, cot_ref, lse_ref, delta_ref, kv_ref, dq_ref, dkv_ref, q_all, cot_all):
    score_scale = HD ** (-0.5)
    me = lax.axis_index("ctx")
    tokens = q_ref.shape[0]
    heads = q_ref.shape[1] // HD
    blocks_here = tokens // BLK
    first = me * blocks_here
    for h in range(heads):
        q_all[h * tokens : (h + 1) * tokens, :] = q_ref[:, h * HD : (h + 1) * HD]
        cot_all[h * tokens : (h + 1) * tokens, :] = cot_ref[:, h * HD : (h + 1) * HD]
    dq_ref[...] = jnp.zeros_like(dq_ref)
    lane = lax.broadcasted_iota(jnp.int32, (1, tokens), 1)
    row_pos = me * tokens + lane
    row_block = row_pos // BLK
    mine = pl.ds(pl.multiple_of(me * tokens, tokens), tokens)

    def block(owner):
        q, cot = (q_all[...], None), (cot_all[...], None)
        k, v = (kv_ref[owner][:, :HD], None), (kv_ref[owner][:, HD:], None)
        key_pos = owner * tokens + lax.broadcasted_iota(jnp.int32, (tokens, tokens), 0)
        key_block = key_pos // BLK
        own = (key_block == row_block) & (key_pos <= row_pos)
        before = key_block < row_block
        scores = mm(k, q, 1, 1)
        dprobs = mm(v, cot, 1, 1)
        probs, dscores = [], []
        for h in range(heads):
            member = None
            for t in range(TOPK):
                entry = jnp.zeros((1, tokens), jnp.int32)
                for b in range(blocks_here):
                    listed = lists_ref[h, t, first + b]
                    entry = jnp.where(lane // BLK == b, listed, entry)
                hit = key_block == entry
                member = hit if member is None else member | hit
            allowed = own | (before & member)
            span = slice(h * tokens, (h + 1) * tokens)
            lse, delta = lse_ref[h : h + 1, mine], delta_ref[h : h + 1, mine]
            prob = jnp.where(allowed, jnp.exp(scores[:, span] * score_scale - lse), 0.0)
            probs.append(prob)
            dscores.append(prob * (dprobs[:, span] - delta) * score_scale)
        ds = split(jnp.concatenate(dscores, axis=1))
        dkv_ref[owner, :, :HD] = mm(ds, q)
        dkv_ref[owner, :, HD:] = mm(split(jnp.concatenate(probs, axis=1)), cot)
        dq = mm(ds, k, 0, 0)
        for h in range(heads):
            dq_ref[:, h * HD : (h + 1) * HD] += dq[h * tokens : (h + 1) * tokens]

    return block


def through_chain(
    lists_ref, aq_hbm, acot_hbm, lse_hbm, delta_hbm, ak_hbm, av_hbm,
    q_hbm, k_hbm, v_hbm, cot_hbm, decay_hbm, write_hbm, rate_ref, scale_ref,
    dq_ref, adk_ref, adv_ref, gdq_ref, gdk_ref, gdv_ref, ddecay_ref, dwrite_ref,
    inv_ref, wu_ref, gam_ref, beta_ref, mem_ref, grad_ref,
    q_ref, k_ref, v_ref, cot_ref, decay_ref, write_ref,
    aq_ref, acot_ref, lse_ref, delta_ref, ak_ref, av_ref, load_sem,
    map_ref, mapt_ref, add_ref, pull_ref, kv, q_all, cot_all, dkv, twin_in, far_in, groups,
    mem_out, grad_out, far_send, far_recv, near_send, near_recv,
    mem_send, mem_recv, grad_send, grad_recv, pair_send, pair_recv, sum_send, sum_recv,
    group_send, group_recv,
):
    n = lax.axis_size("ctx")
    me, head_at = lax.axis_index("ctx"), lax.axis_index("head")
    heads = aq_ref.shape[1] // HD
    chips = n // 2
    loads = [
        pltpu.make_async_copy(source, target, load_sem.at[i])
        for i, (source, target) in enumerate(
            (
                (ak_hbm, ak_ref), (av_hbm, av_ref),
                (q_hbm, q_ref), (k_hbm, k_ref), (v_hbm, v_ref), (cot_hbm, cot_ref),
                (decay_hbm, decay_ref), (write_hbm, write_ref),
                (aq_hbm, aq_ref), (acot_hbm, acot_ref), (lse_hbm, lse_ref), (delta_hbm, delta_ref),
            )
        )
    ]
    for load in loads:
        load.start()
    twin = me + 1 - 2 * lax.rem(me, 2)
    barrier = pltpu.get_barrier_semaphore()
    for d in range(1, n):
        pl.semaphore_signal(
            barrier, inc=1, device_id=(lax.rem(me + d, n), head_at), device_id_type=MESH
        )
    others = lax.axis_size("head")
    for d in range(1, others):
        pl.semaphore_signal(
            barrier, inc=1, device_id=(me, lax.rem(head_at + d, others)), device_id_type=MESH
        )
    for load in loads[:2]:
        load.wait()
    pl.semaphore_wait(barrier, n + others - 2)

    group = head_at * heads // (Q_HEADS // KV_HEADS)
    columns = pl.ds(pl.multiple_of(group * HD, HD), HD)
    kv[me, :, :HD] = ak_ref[:, columns]
    kv[me, :, HD:] = av_ref[:, columns]

    def copy(slot, send_sem, recv_sem, index, to):
        return pltpu.make_async_remote_copy(
            src_ref=kv.at[slot],
            dst_ref=kv.at[slot],
            send_sem=send_sem.at[index],
            recv_sem=recv_sem.at[index],
            device_id=(to, head_at),
            device_id_type=MESH,
        )

    def source(d):
        return lax.rem(me + n - 2 * d, n)

    def far(d):
        return copy(me, far_send, far_recv, d, lax.rem(me + 2 * d, n))

    for d in range(1, chips):
        far(d).start()
    copy(me, near_send, near_recv, 0, twin).start()
    for load in loads[2:8]:
        load.wait()

    gdn_local(
        q_ref, k_ref, v_ref, cot_ref, decay_ref, write_ref, rate_ref, scale_ref,
        inv_ref, wu_ref, map_ref, mapt_ref, add_ref, pull_ref, gam_ref, beta_ref,
    )
    for load in loads[8:]:
        load.wait()
    block = attention(
        lists_ref, aq_ref, acot_ref, lse_ref, delta_ref, kv, dq_ref, dkv, q_all, cot_all
    )
    for d in range(1, chips):
        copy(source(d), far_send, far_recv, d, twin).wait_recv()
        copy(source(d), near_send, near_recv, d, twin).start()

    chip, core = lax.div(me, 2), lax.rem(me, 2)

    def pair(c):
        return pltpu.make_async_remote_copy(
            src_ref=dkv.at[2 * c + 1 - core],
            dst_ref=twin_in.at[c],
            send_sem=pair_send.at[c],
            recv_sem=pair_recv.at[c],
            device_id=(twin, head_at),
            device_id_type=MESH,
        )

    def down(c):
        return pltpu.make_async_remote_copy(
            src_ref=dkv.at[2 * c + core],
            dst_ref=far_in.at[chip - c],
            send_sem=sum_send.at[chip - c],
            recv_sem=sum_recv.at[chip - c],
            device_id=(2 * c + core, head_at),
            device_id_type=MESH,
        )

    def visit(start, to_twin):
        def turn(c, carry):
            owner = 2 * c + lax.rem(start, 2)

            @pl.when(owner <= me)
            def _():
                block(owner)
                if to_twin:
                    pair(c).start()

            return carry

        lax.fori_loop(0, chips, turn, 0)

    visit(me, False)
    for d in range(chips):
        copy(lax.rem(twin + n - 2 * d, n), near_send, near_recv, d, twin).wait_recv()
    visit(twin, True)

    def combine(c, carry):
        @pl.when(2 * c + core <= twin)
        def _():
            pair(c).wait_recv()
            dkv[2 * c + core] = dkv[2 * c + core] + twin_in[c]

        return carry

    lax.fori_loop(0, chips, combine, 0)

    def send_down():
        def turn(c, carry):
            @pl.when(c < chip)
            def _():
                down(c).start()

            return carry

        lax.fori_loop(0, chips, turn, 0)

    early = 2 * chip < chips

    @pl.when(early)
    def _():
        send_down()

    def share(d):
        return pltpu.make_async_remote_copy(
            src_ref=groups.at[head_at],
            dst_ref=groups.at[head_at],
            send_sem=group_send.at[d],
            recv_sem=group_recv.at[d],
            device_id=(me, lax.rem(head_at + d, others)),
            device_id_type=MESH,
        )

    def finish_sum():
        groups[head_at] = dkv[me]

        def turn(d, carry):
            @pl.when(chip + d < chips)
            def _():
                pltpu.make_async_remote_copy(
                    src_ref=dkv.at[me],
                    dst_ref=far_in.at[d],
                    send_sem=sum_send.at[d],
                    recv_sem=sum_recv.at[d],
                    device_id=(twin, head_at),
                    device_id_type=MESH,
                ).wait_recv()
                groups[head_at] = groups[head_at] + far_in[d]

            return carry

        lax.fori_loop(1, chips, turn, 0)
        for d in range(1, others):
            share(d).start()

    right, left = lax.rem(me + 1, n), lax.rem(me + n - 1, n)
    value_heads = map_ref.shape[0]

    def send(source, target, send_sem, recv_sem, head, to):
        return pltpu.make_async_remote_copy(
            src_ref=source.at[head],
            dst_ref=target.at[head],
            send_sem=send_sem.at[head],
            recv_sem=recv_sem.at[head],
            device_id=(to, head_at),
            device_id_type=MESH,
        )

    def advance(head):
        copy = send(mem_out, mem_ref, mem_send, mem_recv, head, right)

        @pl.when(me == 0)
        def _():
            mem_ref[head] = jnp.zeros((GDIM, GDIM), F32)

        @pl.when(me > 0)
        def _():
            copy.wait_recv()

        @pl.when(me < n - 1)
        def _():
            mem_out[head] = mm(split(map_ref[head]), split(mem_ref[head])) + add_ref[head]
            copy.start()

    def retreat(head):
        copy = send(grad_out, grad_ref, grad_send, grad_recv, head, left)

        @pl.when(me == n - 1)
        def _():
            grad_ref[head] = jnp.zeros((GDIM, GDIM), F32)

        @pl.when(me < n - 1)
        def _():
            copy.wait_recv()

        @pl.when(me > 0)
        def _():
            grad_out[head] = mm(split(mapt_ref[head]), split(grad_ref[head])) + pull_ref[head]
            copy.start()

    steps = 2 * value_heads
    lag = jnp.clip((n - 1 - 2 * me) * 3, -value_heads, value_heads)
    mem_late, grad_late = jnp.maximum(-lag, 0), jnp.maximum(lag, 0)

    def turn(step, carry):
        mem_head, grad_head = step - mem_late, step - grad_late

        @pl.when((mem_head >= 0) & (mem_head < value_heads))
        def _():
            advance(mem_head)

        @pl.when((grad_head >= 0) & (grad_head < value_heads))
        def _():
            retreat(grad_head)

        @pl.when((step == value_heads - 1) & jnp.logical_not(early))
        def _():
            send_down()

        return carry

    lax.fori_loop(0, steps, turn, 0)

    def after_head(m):
        @pl.when(sum_slot == m + 1)
        def _():
            finish_sum()

    sum_slot = jnp.minimum(chips - 1 - chip, q_ref.shape[1] // GDIM)
    after_head(-1)
    gdn_grads(
        q_ref, k_ref, v_ref, cot_ref, decay_ref, write_ref, rate_ref, scale_ref,
        inv_ref, wu_ref, gam_ref, beta_ref, mem_ref, grad_ref,
        gdq_ref, gdk_ref, gdv_ref, ddecay_ref, dwrite_ref, after_head,
    )

    def drain(head, carry):
        @pl.when(me < n - 1)
        def _():
            send(mem_out, mem_ref, mem_send, mem_recv, head, right).wait_send()

        @pl.when(me > 0)
        def _():
            send(grad_out, grad_ref, grad_send, grad_recv, head, left).wait_send()

        return carry

    lax.fori_loop(0, value_heads, drain, 0)

    def drain_sums(c, carry):
        @pl.when(2 * c + 1 - core <= me)
        def _():
            pair(c).wait_send()

        @pl.when(c < chip)
        def _():
            down(c).wait_send()

        return carry

    lax.fori_loop(0, chips, drain_sums, 0)
    for d in range(1, others):
        here = lax.rem(head_at + others - d, others)
        pltpu.make_async_remote_copy(
            src_ref=groups.at[here],
            dst_ref=groups.at[here],
            send_sem=group_send.at[d],
            recv_sem=group_recv.at[d],
            device_id=(me, here),
            device_id_type=MESH,
        ).wait_recv()
    each = others // KV_HEADS
    for c in range(KV_HEADS):
        total = groups[c * each]
        for d in range(1, each):
            total = total + groups[c * each + d]
        adk_ref[:, c * HD : (c + 1) * HD] = total[:, :HD]
        adv_ref[:, c * HD : (c + 1) * HD] = total[:, HD:]
    for d in range(1, others):
        share(d).wait_send()
    for d in range(1, chips):
        far(d).wait_send()
    for d in range(chips):
        copy(source(d), near_send, near_recv, d, twin).wait_send()


def hand_over(*refs):
    count = len(refs) // 2
    for i in range(count):
        refs[count + i][...] = refs[i][...]


def on_device(
    attn_q, attn_k, attn_v, attn_cot, attn_lse, attn_delta, block_lists,
    gdn_q, gdn_k, gdn_v, decay_logit, write_logit, decay_rate, write_scale, gdn_cot,
):
    tokens = attn_q.shape[0]
    local_heads = attn_q.shape[1] // HD
    ctx = lax.axis_size("ctx")
    head_devices = lax.axis_size("head")
    value_heads = gdn_v.shape[1] // GDIM
    vmem, smem = (pl.BlockSpec(memory_space=space) for space in (pltpu.VMEM, pltpu.SMEM))

    gates = jax.ShapeDtypeStruct((value_heads, tokens), F32)
    key_grads = jax.ShapeDtypeStruct((tokens, KV_HEADS * HD), F32)
    buffer = pltpu.VMEM((value_heads, GDIM, GDIM), F32)
    stacked = pltpu.VMEM((local_heads * tokens, HD), BF16)

    def sums(count, kind):
        return pltpu.VMEM((count, tokens, 2 * HD), kind)

    def sems(count):
        return pltpu.SemaphoreType.DMA((count,))

    attn_in = (attn_q, attn_cot, attn_lse, attn_delta, attn_k, attn_v)
    gdn_in = (gdn_q, gdn_k, gdn_v, gdn_cot, decay_logit, write_logit)
    chips = ctx // 2
    hbm = pl.BlockSpec(memory_space=pltpu.HBM)
    results = (
        jax.ShapeDtypeStruct(attn_q.shape, F32),
        key_grads, key_grads,
        *(jax.ShapeDtypeStruct(x.shape, F32) for x in (gdn_q, gdn_k, gdn_v)),
        gates, gates,
    )
    held = pl.pallas_call(
        through_chain,
        out_shape=results,
        in_specs=[smem] + [hbm] * 12 + [smem, smem],
        out_specs=[vmem] * 8,
        scratch_shapes=[
            pltpu.VMEM((value_heads, tokens, tokens), F32),
            pltpu.VMEM((value_heads, tokens, 2 * GDIM), F32),
            pltpu.VMEM(gates.shape, F32),
            pltpu.VMEM(gates.shape, F32),
            buffer, buffer,
        ]
        + [pltpu.VMEM(x.shape, x.dtype) for x in gdn_in + attn_in]
        + [sems(12)]
        + [buffer] * 4
        + [sums(ctx, BF16), stacked, stacked, sums(ctx, F32), sums(chips, F32), sums(chips, F32)]
        + [sums(head_devices, F32), buffer, buffer]
        + [sems(chips)] * 4
        + [sems(value_heads)] * 4
        + [sems(chips)] * 4
        + [sems(head_devices)] * 2,
        compiler_params=pltpu.CompilerParams(
            collective_id=0, has_side_effects=True, vmem_limit_bytes=VMEM_BYTES
        ),
        name="through_chain",
    )(block_lists.transpose(0, 2, 1), *attn_in, *gdn_in, decay_rate, write_scale)

    return pl.pallas_call(
        hand_over,
        out_shape=results,
        in_specs=[vmem] * len(results),
        out_specs=[vmem] * len(results),
        compiler_params=pltpu.CompilerParams(vmem_limit_bytes=VMEM_BYTES),
        name="hand_over",
    )(*held)


def solution(mesh):
    return jax.shard_map(
        on_device,
        mesh=mesh,
        in_specs=(
            P("ctx", "head"), P("ctx", None), P("ctx", None), P("ctx", "head"),
            P("head", None), P("head", None), P("head", None, None),
            P("ctx", "head"), P("ctx", "head"), P("ctx", "head"),
            P("head", "ctx"), P("head", "ctx"), P("head"), P("head"), P("ctx", "head"),
        ),
        out_specs=(
            P("ctx", "head"), P("ctx", None), P("ctx", None),
            P("ctx", "head"), P("ctx", "head"), P("ctx", "head"),
            P("head", "ctx"), P("head", "ctx"),
        ),
        check_vma=False,
    )
```
